128 devices in a mesh: outer: 4 (over x), inner: 32 (over z, y, core).
Axes of the slice: x: 4, y: 4, z: 4, core: 2. Of those that a mesh axis runs over, the one named last changes fastest.
Arguments:
- tokens: bfloat16 [16384, 1024], P(('outer', 'inner')), may hold values from -200 to 200
- out_grad: bfloat16 [16384, 1024], P(('outer', 'inner')), may hold values from -30 to 30
- query_weight: bfloat16 [1024, 1024], replicated, may hold values from -0.1875 to 0.1875
- gain: float32 [1024], replicated, may hold values from 0.1 to 1.9
- shift: float32 [1024], replicated, may hold values from -3 to 3
- first_keys: bfloat16 [2, 512, 256], replicated, may hold values from -0.65 to 0.65
- second_keys: bfloat16 [2, 512, 256], replicated, may hold values from -0.65 to 0.65
- values: bfloat16 [2, 262144, 1024], P(None, ('outer', 'inner')), may hold values from -6 to 6
- pick_shard: int32 [16384, 2, 16], P(('outer', 'inner')), may hold values from 0 to 127, all different within a row; in each aligned block of 256 rows (0 to 255, 256 to 511, ..., all dimensions but the last counted through in order) at most 40 rows name the same one
- pick_low: int32 [16384, 2, 16], P(('outer', 'inner')), may hold values from 0 to 3
- pick_second: int32 [16384, 2, 16], P(('outer', 'inner')), may hold values from 0 to 511
Outputs:
- token_grad: bfloat16 [16384, 1024], P(('outer', 'inner'))
- query_weight_grad: float32 [1024, 1024], P(('outer', 'inner'))
- gain_grad: float32 [1024], replicated
- shift_grad: float32 [1024], replicated
- first_key_grad: float32 [2, 512, 256], replicated
- second_key_grad: float32 [2, 512, 256], replicated
- value_grad: bfloat16 [2, 262144, 1024], P(None, ('outer', 'inner'))
The draws below stay inside these ranges and needn't reach their ends.
Inputs may be any that keep to these rules, and one draw needn't show every extreme that they name: `pick_shard`: the 16 picks of one token and head name 16 different shards; among the picks of one device's tokens no shard is named more than 40 times, and in some device's tokens one is named exactly 40 times.
All inputs are finite; a program needn't handle non-finite values.
Results may differ from the reference program's by a relative error of at most 0.01.
The reference program's roundings to bfloat16 on the way (of `query`, `message` and `raw_grad`) count: a program that leaves them out, or rounds other values in their place, can miss the bound.
Values may be sent and summed in bfloat16 or wider, within the bound.
No kernel may reach another device: no remote copies, remote signals or barrier semaphores. Data moves between devices by JAX's collectives and lax.ppermute only.
A program may use at most 128 MiB of HBM per device.

```python
import math
import jax
import jax.numpy as jnp
import numpy as np
from jax import lax

D = 1024
HEADS = 2
KDIM = 512
SUBKEYS = 512
TOPK = 16
TOK_DEV = 128
HALF = 256
ROWS = 262144
FIRST_DEV = 4
TOKENS = 16384
MOST = 40
DEVICES = 128


def sign_pattern(key):
    return 2.0 * jax.random.bernoulli(key, 0.5, (HEADS, KDIM)).astype(jnp.float32) - 1.0


def draw_tokens(key, part):
    key = jax.random.fold_in(key, 11)
    key_rows, key_columns, key_sample = jax.random.split(key, 3)
    growth = 1.0 + 2.0 * jnp.arange(TOKENS, dtype=jnp.float32) / (TOKENS - 1)
    row_scale = jnp.exp(jax.random.uniform(key_rows, (TOKENS, 1), minval=0.0, maxval=math.log(10.0))) / 3.0
    column_scale = jnp.exp(jax.random.uniform(key_columns, (1, D), minval=0.0, maxval=math.log(10.0))) / 3.0
    sample = jnp.clip(jax.random.normal(key_sample, (TOKENS, D)), -6.0, 6.0) * row_scale
    return (sample * column_scale * growth[:, None]).astype(jnp.bfloat16)


def draw_out_grad(key, part):
    key = jax.random.fold_in(key, 12)
    key_rows = jax.random.fold_in(key, 0)
    key_sample = jax.random.fold_in(key, 2)
    growth = 1.0 + 2.0 * jnp.arange(TOKENS, dtype=jnp.float32) / (TOKENS - 1)
    row_scale = jnp.exp(jax.random.uniform(key_rows, (TOKENS, 1), minval=0.0, maxval=math.log(4.0))) / 2.0
    sample = jnp.clip(jax.random.normal(key_sample, (TOKENS, D)), -4.0, 4.0) * row_scale
    return (sample * growth[:, None]).astype(jnp.float32).astype(jnp.bfloat16)


def draw_shift(key, part):
    pattern = sign_pattern(key).reshape(-1)
    key = jax.random.fold_in(key, 13)
    return jnp.clip(0.5 * jax.random.normal(key, pattern.shape), -2.5, 2.5)


def draw_first_keys(key, part):
    key = jax.random.fold_in(key, 14)
    return jnp.clip(0.13 * jax.random.normal(key, (HEADS, SUBKEYS, HALF)), -0.52, 0.52).astype(jnp.bfloat16)


def draw_second_keys(key, part):
    key = jax.random.fold_in(key, 15)
    return jnp.clip(0.13 * jax.random.normal(key, (HEADS, SUBKEYS, HALF)), -0.52, 0.52).astype(jnp.bfloat16)


def set_ends(result, stream_key, least, high):
    extent = result.shape
    place = [jax.random.randint(jax.random.fold_in(stream_key, axis), (), 0, extent[axis]) for axis in range(len(extent))]
    result = result.at[tuple(place)].set(least)
    longest = extent.index(max(extent))
    place[longest] = (place[longest] + 1) % extent[longest]
    return result.at[tuple(place)].set(high)


def shard_levels(rng, shape, cuts, least, top_value):
    level, own = 1.0, jax.random.fold_in(rng, 6)
    for axis_at, parts in cuts:
        heights = jnp.exp(jax.random.uniform(jax.random.fold_in(own, axis_at), (parts,), jnp.float32, least / len(cuts), top_value / len(cuts)))
        level = level * jnp.repeat(heights, shape[axis_at] // parts).reshape([-1 if axis == axis_at else 1 for axis in range(len(shape))])
    return level


def deal_out(stream_key, own, number, rows, count, top, limit, slope):
    ranking = jax.random.permutation(stream_key, count)
    packed, usual = load_shares(count, rows * top, limit, slope, True), load_shares(count, rows * top, limit, slope, False)
    places = jnp.arange(count)

    def named(lengths, rotation):
        used = int((lengths > 0).sum())
        fixed = max(1, used // 4)
        passed = fixed + (places - fixed + rotation * (used - fixed)) % max(1, count - fixed)
        return jnp.zeros((count,), jnp.int32).at[ranking[jnp.where(places < fixed, places, passed)]].set(jnp.asarray(lengths, jnp.int32))

    lengths = jnp.where(number % 4 == 0, named(packed, number // 4), named(usual, number - number // 4 - 1))
    mixed = jax.random.permutation(jax.random.fold_in(own, 3), count)
    source_of, receiver = mixed[0:count // 2 * 2:2], mixed[1:count // 2 * 2:2]
    room = jnp.minimum(lengths[source_of] - 1, limit - lengths[receiver]) // 2
    room = jnp.where((source_of == ranking[0]) | (receiver == ranking[0]) | (lengths[receiver] == 0), 0, jnp.maximum(room, 0))
    passed = jax.random.randint(jax.random.fold_in(own, 4), (count // 2,), 0, 1 << 20) % (room + 1)
    lengths = lengths.at[source_of].add(-passed).at[receiver].add(passed)
    members = jnp.searchsorted(jnp.cumsum(lengths), jnp.arange(rows * top), side="right").astype(jnp.int32)
    grid = members.reshape(top, rows).T
    grid = grid[jax.random.permutation(jax.random.fold_in(own, 1), rows)]
    rotation = jax.random.randint(jax.random.fold_in(own, 2), (rows, 1), 0, top)
    return jnp.take_along_axis(grid, (jnp.arange(top)[None, :] + rotation) % top, axis=1)


def load_shares(number_of, total, reach, slope, full):
    loads = [(1 << 20) // math.isqrt(grade ** slope) + 1 for grade in range(1, number_of + 1)]
    largest = reach if full else min(reach, max(-(-total // number_of), total * loads[0] // sum(loads)))
    least = 1 if total - largest >= number_of - 1 else 0
    holding, surplus = [largest] + [least] * (number_of - 1), total - largest - least * (number_of - 1)
    while surplus > 0:
        free = [i for i in range(1, number_of) if holding[i] < largest] or [i for i in range(1, number_of) if holding[i] < reach]
        mass, remaining = sum([loads[i] for i in free]), surplus
        for i in free:
            addition = min(reach - holding[i], max(1, remaining * loads[i] // mass), surplus)
            holding[i] = holding[i] + addition
            surplus = surplus - addition
    return np.array(holding)


def gaussian(own_key, dims, scale, reach, pieces=(), kind=jnp.bfloat16):
    values = jax.random.normal(own_key, dims, jnp.float32) * scale
    if len(pieces) > 0:
        values = shard_levels(own_key, dims, pieces, -0.22, 0.18) * values
    return jnp.clip(values, min=-reach, max=reach).astype(kind)


def setup_inputs(seed: int = 0) -> dict:
    key_of = jax.random.split(jax.random.key(seed), 12)
    tokens = draw_tokens(jax.random.fold_in(key_of[11], 71), 0)
    out_grad = draw_out_grad(jax.random.fold_in(key_of[11], 71), 0)
    query_weight = gaussian(key_of[2], (D, HEADS * KDIM), D ** -0.5, 0.1875)
    gain = jnp.clip(1.0 + 0.18 * jax.random.normal(key_of[3], (HEADS * KDIM,), jnp.float32), 0.1, 1.9)
    shift = draw_shift(jax.random.fold_in(key_of[11], 71), 0)
    first_keys = draw_first_keys(jax.random.fold_in(key_of[11], 71), 0)
    second_keys = draw_second_keys(jax.random.fold_in(key_of[11], 71), 0)
    values = gaussian(key_of[7], (HEADS, ROWS, D), 1.0, 6.0, ((1, 128),))
    pick_shard_keys = jax.random.split(jax.random.fold_in(key_of[8], 1), TOKENS * HEADS // (TOK_DEV * HEADS))
    pick_shard_turns = jax.random.permutation(jax.random.fold_in(key_of[8], 3), TOKENS * HEADS // (TOK_DEV * HEADS))
    pick_shard = jax.vmap(lambda own, number: deal_out(jax.random.fold_in(key_of[8], 2), own, number, TOK_DEV * HEADS, DEVICES, TOPK, MOST, 2))(pick_shard_keys, pick_shard_turns).reshape((TOKENS, HEADS, TOPK))
    pick_low = set_ends(jax.random.randint(key_of[9], (TOKENS, HEADS, TOPK), 0, FIRST_DEV), jax.random.fold_in(key_of[9], 1), 0, FIRST_DEV - 1).astype(jnp.int32)
    pick_second = set_ends(jax.random.randint(key_of[10], (TOKENS, HEADS, TOPK), 0, SUBKEYS), jax.random.fold_in(key_of[10], 1), 0, SUBKEYS - 1).astype(jnp.int32)
    return dict(tokens=tokens, out_grad=out_grad, query_weight=query_weight, gain=gain, shift=shift, first_keys=first_keys, second_keys=second_keys, values=values, pick_shard=pick_shard, pick_low=pick_low, pick_second=pick_second)


epsilon = 1e-05

def value_pass(out_grad, values_head, pick_weight, row_ids):
    block_rows = math.gcd(TOKENS, 512)
    block_count = TOKENS // block_rows

    def scan_block(accumulated, block_data):
        grad_block, weight_block, row_block = block_data
        message = (weight_block[:, :, None] * grad_block[:, None, :].astype(jnp.float32)).astype(jnp.bfloat16)
        message = lax.optimization_barrier(message)
        fetched = values_head[row_block]
        products = lax.optimization_barrier(jnp.sum(message.astype(jnp.float32) * fetched.astype(jnp.float32), axis=-1))
        accumulated = accumulated.at[row_block.reshape(-1)].add(message.reshape(-1, D).astype(jnp.float32))
        return (accumulated, products)
    initial = jnp.zeros((ROWS, D), jnp.float32)
    accumulated, products = lax.scan(scan_block, initial, (out_grad.reshape(block_count, block_rows, D), pick_weight.reshape(block_count, block_rows, TOPK), row_ids.reshape(block_count, block_rows, TOPK)))
    return (accumulated.astype(jnp.bfloat16), products.reshape(TOKENS, TOPK))

def reference(tokens, out_grad, query_weight, gain, shift, first_keys, second_keys, values, pick_shard, pick_low, pick_second):
    raw_query = jnp.dot(tokens, query_weight, preferred_element_type=jnp.float32)
    centre = lax.optimization_barrier(jnp.sum(raw_query, axis=0)) / TOKENS
    shifted = raw_query - centre
    spread = lax.optimization_barrier(jnp.sum(shifted * shifted, axis=0)) / TOKENS
    inverse = 1.0 / jnp.sqrt(spread + epsilon)
    normed = shifted * inverse
    query = (normed * gain + shift).astype(jnp.bfloat16).reshape(TOKENS, HEADS, KDIM)
    first_index = (pick_shard * FIRST_DEV + pick_low).astype(jnp.int32)
    token_ids = jnp.arange(TOKENS, dtype=jnp.int32)[:, None]
    query_parts = []
    first_parts = []
    second_parts = []
    value_parts = []
    for head_id in range(HEADS):
        near_query = query[:, head_id, :HALF]
        far_query = query[:, head_id, HALF:]
        near_full = jnp.dot(near_query, first_keys[head_id].T, preferred_element_type=jnp.float32)
        far_full = jnp.dot(far_query, second_keys[head_id].T, preferred_element_type=jnp.float32)
        score = jnp.take_along_axis(near_full, first_index[:, head_id], axis=1) + jnp.take_along_axis(far_full, pick_second[:, head_id], axis=1)
        pick_weight = jax.nn.softmax(score, axis=-1)
        row_ids = (first_index[:, head_id] * SUBKEYS + pick_second[:, head_id]).astype(jnp.int32)
        value_grad, products = value_pass(out_grad, values[head_id], pick_weight, row_ids)
        score_grad = products - pick_weight * lax.optimization_barrier(jnp.sum(products, axis=-1, keepdims=True))
        near_dense = jnp.zeros((TOKENS, SUBKEYS), jnp.float32).at[token_ids, first_index[:, head_id]].add(score_grad)
        far_dense = jnp.zeros((TOKENS, SUBKEYS), jnp.float32).at[token_ids, pick_second[:, head_id]].add(score_grad)
        query_parts.append(jnp.dot(near_dense, first_keys[head_id].astype(jnp.float32), precision=lax.Precision.HIGHEST))
        query_parts.append(jnp.dot(far_dense, second_keys[head_id].astype(jnp.float32), precision=lax.Precision.HIGHEST))
        first_parts.append(jnp.dot(near_dense.T, near_query.astype(jnp.float32), precision=lax.Precision.HIGHEST))
        second_parts.append(jnp.dot(far_dense.T, far_query.astype(jnp.float32), precision=lax.Precision.HIGHEST))
        value_parts.append(value_grad)
    query_grad = jnp.concatenate(query_parts, axis=1)
    shift_grad = lax.optimization_barrier(jnp.sum(query_grad, axis=0))
    gain_grad = lax.optimization_barrier(jnp.sum(query_grad * normed, axis=0))
    raw_grad = (gain * inverse * (query_grad - shift_grad / TOKENS - normed * gain_grad / TOKENS)).astype(jnp.bfloat16)
    token_grad = jnp.dot(raw_grad, query_weight.T, preferred_element_type=jnp.float32).astype(jnp.bfloat16)
    query_weight_grad = jnp.dot(raw_grad.T, tokens, preferred_element_type=jnp.float32)
    return (token_grad, query_weight_grad, gain_grad, shift_grad, jnp.stack(first_parts), jnp.stack(second_parts), jnp.stack(value_parts))
```

```python
import functools
import jax
import jax.numpy as jnp
from jax import lax
from jax.experimental import pallas as pl
from jax.experimental.pallas import tpu as pltpu
from jax.sharding import Mesh, PartitionSpec as P

epsilon = 1e-05
F32, BF16, I32 = jnp.float32, jnp.bfloat16, jnp.int32
ALL = ("x", "z", "y", "c")
CHIPS = ("x", "z", "y")
CAP = 40
GROUP = 8
LANES = 128
NT = (((1,), (1,)), ((), ()))
TN = (((0,), (0,)), ((), ()))


def iota(shape, axis):
    return lax.broadcasted_iota(I32, shape, axis)


def slot_table(pos, payload):
    lines = []
    for j in range(CAP):
        found = sum(jnp.where(p == j, v, jnp.zeros_like(v)) for p, v in zip(pos, payload))
        lines.append(jnp.sum(found, axis=0, keepdims=True))
    lines.append(jnp.zeros((LANES - CAP, LANES), payload[0].dtype))
    return lines


def slots_kernel(heads, top, shard_ref, code_ref, pos_ref, dense_ref, slot_ref):
    n = shard_ref.shape[0]
    lane = iota((n, LANES), 1)
    row = iota((n, LANES), 0)
    below = (iota((n, n), 1) < iota((n, n), 0)).astype(BF16)
    before = jnp.zeros((1, LANES), F32)
    pos, packed = [], []
    for h in range(heads):
        code = jnp.full((n, LANES), -1, I32)
        for k in range(top):
            at = h * top + k
            code = jnp.where(shard_ref[:, at : at + 1] == lane, code_ref[:, at : at + 1], code)
        hit = code >= 0
        ones = jnp.where(hit, 1.0, 0.0)
        place = jnp.dot(below, ones.astype(BF16), preferred_element_type=F32) + before
        before = before + jnp.sum(ones, axis=0, keepdims=True)
        place = jnp.where(hit, place, -1.0)
        pos.append(place)
        packed.append(((h * 2048 + code) * n + row).astype(F32))
        pos_ref[h * n : (h + 1) * n, :] = place
        dense_ref[h * n : (h + 1) * n, :] = code
    lines = slot_table(pos, packed)
    table = jnp.concatenate(lines[:CAP] + [before, lines[CAP][1:]], axis=0)
    slot_ref[...] = table.T.astype(I32)


def score_kernel(
    heads, half, raw_ref, stat_ref, gain_ref, shift_ref, first_ref, second_ref, pos_ref, dense_ref,
    query_ref, normed_ref, weight_ref, slot_ref,
):
    n = raw_ref.shape[0]
    normed = (raw_ref[...] - stat_ref[0:1, :]) * stat_ref[1:2, :]
    normed_ref[...] = normed
    query = (normed * gain_ref[...] + shift_ref[...]).astype(BF16)
    query_ref[...] = query
    pos, weights = [], []
    for h in range(heads):
        code = dense_ref[h * n : (h + 1) * n, :]
        hit = code >= 0
        low = code >> 9
        second = jnp.maximum(code, 0) & 511
        base = h * 2 * half
        near = query[:, base : base + half]
        far = query[:, base + half : base + 2 * half]
        score = jnp.zeros((n, LANES), F32)
        for part in range(4):
            dense = lax.dot_general(
                near, first_ref[h, part * LANES : (part + 1) * LANES, :], NT, preferred_element_type=F32
            )
            score = jnp.where(low == part, dense, score)
        found = jnp.zeros((n, LANES), F32)
        for part in range(4):
            dense = lax.dot_general(
                far, second_ref[h, part * LANES : (part + 1) * LANES, :], NT, preferred_element_type=F32
            )
            taken = jnp.take_along_axis(dense, second & (LANES - 1), axis=1)
            found = jnp.where((second >> 7) == part, taken, found)
        score = jnp.where(hit, score + found, -jnp.inf)
        most = jnp.max(score, axis=1, keepdims=True)
        power = jnp.where(hit, jnp.exp(score - most), 0.0)
        weight = power / jnp.sum(power, axis=1, keepdims=True)
        weight_ref[h * n : (h + 1) * n, :] = weight
        pos.append(pos_ref[h * n : (h + 1) * n, :])
        weights.append(weight)
    slot_ref[...] = jnp.concatenate(slot_table(pos, weights), axis=0).T


def serve_kernel(tokens, rows, index_ref, weight_ref, grad_ref, value_ref, out_ref, product_ref, total, held):
    step = pl.program_id(0)

    @pl.when(step == 0)
    def _():
        def clear(i, carry):
            at = pl.multiple_of(i * 256, 256)
            total[pl.ds(at, 256), :] = jnp.zeros((256, LANES), F32)
            return carry

        lax.fori_loop(0, rows * 8 // 256, clear, 0)

    eye = iota((CAP, LANES), 0) == iota((CAP, LANES), 1)

    def one_sender(g, carry):
        sender = step * GROUP + g
        count = index_ref[sender, CAP]

        def eight(b, inner):
            for u in range(8):
                j = b * 8 + u
                packed = index_ref[sender, j]
                weight = weight_ref[sender, j]
                row = packed // tokens
                token = packed % tokens
                grad = grad_ref[g * tokens + token].astype(F32)
                message = (grad * weight).astype(BF16).astype(F32)
                value = value_ref[row].astype(F32)
                held[pl.ds(pl.multiple_of(j * 8, 8), 8), :] = message * value
                at = pl.ds(pl.multiple_of(row * 8, 8), 8)
                total[at, :] += message
            return inner

        lax.fori_loop(0, (count + 7) // 8, eight, 0)
        part = held[pl.ds(0, CAP, stride=8), :]
        for c in range(1, 8):
            part = part + held[pl.ds(c, CAP, stride=8), :]
        summed = jnp.sum(part, axis=1, keepdims=True)
        line = jnp.sum(jnp.where(eye, summed, 0.0), axis=0, keepdims=True)
        product_ref[pl.ds(sender, 1), :] = line
        return carry

    lax.fori_loop(0, GROUP, one_sender, 0)

    @pl.when(step == pl.num_programs(0) - 1)
    def _():
        def emit(i, carry):
            at = pl.multiple_of(i * 16, 16)
            for c in range(8):
                out_ref[pl.ds(at, 16), c * LANES : (c + 1) * LANES] = total[
                    pl.ds(at * 8 + c, 16, stride=8), :
                ].astype(BF16)
            return carry

        lax.fori_loop(0, rows // 16, emit, 0)


def split(value):
    high = value.astype(BF16)
    return high, (value - high.astype(F32)).astype(BF16)


def back_kernel(
    heads, top, half, back_ref, shard_ref, second_ids_ref, pos_ref, dense_ref, weight_ref, query_ref,
    normed_ref, first_ref, second_ref, grad_ref, key_ref, sum_ref,
):
    n = query_ref.shape[0]
    table = back_ref[...].T
    wide = iota((n, 4 * LANES), 1)
    for h in range(heads):
        pos = pos_ref[h * n : (h + 1) * n, :]
        product = jnp.zeros((n, LANES), F32)
        for j in range(CAP):
            product = jnp.where(pos == j, table[j : j + 1, :], product)
        weight = weight_ref[h * n : (h + 1) * n, :]
        score = product - weight * jnp.sum(product, axis=1, keepdims=True)
        code = dense_ref[h * n : (h + 1) * n, :]
        low = code >> 9
        near_dense = jnp.concatenate([jnp.where(low == part, score, 0.0) for part in range(4)], axis=1)
        shards = jnp.concatenate(
            [shard_ref[:, h * top : (h + 1) * top], jnp.zeros((n, LANES - top), I32)], axis=1
        )
        picked = jnp.take_along_axis(score, shards, axis=1)
        far_dense = jnp.zeros((n, 4 * LANES), F32)
        for k in range(top):
            at = h * top + k
            far_dense = far_dense + jnp.where(
                second_ids_ref[:, at : at + 1] == wide, picked[:, k : k + 1], 0.0
            )
        base = h * 2 * half
        for side, dense, keys in ((0, near_dense, first_ref), (1, far_dense, second_ref)):
            cols = slice(base + side * half, base + (side + 1) * half)
            high, rest = split(dense)
            table_h = keys[h]
            grad = jnp.dot(high, table_h, preferred_element_type=F32) + jnp.dot(
                rest, table_h, preferred_element_type=F32
            )
            grad_ref[:, cols] = grad
            sum_ref[0:1, cols] = jnp.sum(grad, axis=0, keepdims=True)
            sum_ref[1:2, cols] = jnp.sum(grad * normed_ref[:, cols], axis=0, keepdims=True)
            query = query_ref[:, cols]
            key_ref[side, h] = lax.dot_general(high, query, TN, preferred_element_type=F32) + lax.dot_general(
                rest, query, TN, preferred_element_type=F32
            )


def call(kernel, out_shape, limit=40, **more):
    return pl.pallas_call(
        kernel,
        out_shape=out_shape,
        compiler_params=pltpu.CompilerParams(vmem_limit_bytes=limit << 20),
        **more,
    )


def shape(dims, dtype):
    return jax.ShapeDtypeStruct(dims, dtype)


def swap_core(value):
    return lax.ppermute(value, "c", [(0, 1), (1, 0)])


def everyone(value, axis):
    size = lax.axis_size(axis)
    wide = jnp.broadcast_to(value[None], (size,) + value.shape)
    return lax.all_to_all(wide, axis, split_axis=0, concat_axis=0, tiled=True)


def all_sum(value):
    value = value + swap_core(value)
    for axis in ("y", "z", "x"):
        value = jnp.sum(everyone(value, axis), axis=0)
    return value


def all_moments(mean, spread, count):
    for axis in ("c", "y", "z", "x"):
        both = jnp.stack([mean, spread])
        parts = jnp.stack([both, swap_core(both)]) if axis == "c" else everyone(both, axis)
        mean = jnp.mean(parts[:, 0], axis=0)
        spread = jnp.sum(parts[:, 1] + count * jnp.square(parts[:, 0] - mean), axis=0)
        count = count * parts.shape[0]
    return mean, spread / count


def pair_halves(blocks):
    core = lax.axis_index("c")
    own = lax.dynamic_index_in_dim(blocks, core, 1, keepdims=False)
    other = lax.dynamic_index_in_dim(blocks, 1 - core, 1, keepdims=False)
    return own + swap_core(other)


def scatter_sum(blocks, dtype):
    chips = pair_halves(blocks).astype(dtype)
    arrived = lax.all_to_all(chips, CHIPS, split_axis=0, concat_axis=0, tiled=True)
    return jnp.sum(arrived.astype(F32), axis=0)


def per_device(
    tokens, out_grad, query_weight, gain, shift, first_keys, second_keys, values, pick_shard, pick_low,
    pick_second,
):
    devices = lax.axis_size(ALL)
    n = tokens.shape[0]
    heads, rows_dev, width = values.shape
    subkeys, half = first_keys.shape[1:]
    top = pick_shard.shape[2]
    everything = n * devices
    rows = heads * rows_dev

    tiles = out_grad.reshape(n, 8, width // 8)
    all_grad = lax.all_gather(tiles, ALL, axis=0, tiled=True)

    raw_query = jnp.dot(tokens, query_weight, preferred_element_type=F32)
    local_mean = jnp.mean(raw_query, axis=0)
    local_spread = jnp.sum(jnp.square(raw_query - local_mean), axis=0)
    centre, spread = all_moments(local_mean, local_spread, n)
    inverse = 1.0 / jnp.sqrt(spread + epsilon)

    shard_ids = pick_shard.reshape(n, heads * top)
    second_ids = pick_second.reshape(n, heads * top)
    code = pick_low.reshape(n, heads * top) * subkeys + second_ids
    pos, dense, slot_index = call(
        functools.partial(slots_kernel, heads, top),
        (shape((heads * n, LANES), F32), shape((heads * n, LANES), I32), shape((devices, LANES), I32)),
    )(shard_ids, code)
    slot_index = lax.all_to_all(slot_index.reshape(devices, 1, LANES), ALL, split_axis=0, concat_axis=0, tiled=True)

    first_split = first_keys.reshape(heads, devices, subkeys // devices, half).swapaxes(1, 2)
    first_split = first_split.reshape(heads, subkeys, half)
    query, normed, weight, slot_weight = call(
        functools.partial(score_kernel, heads, half),
        (
            shape((n, width), BF16),
            shape((n, width), F32),
            shape((heads * n, LANES), F32),
            shape((devices, LANES), F32),
        ),
    )(
        raw_query, jnp.stack([centre, inverse]), gain[None], shift[None], first_split, second_keys, pos, dense
    )
    slot_weight = lax.all_to_all(slot_weight.reshape(devices, 1, LANES), ALL, split_axis=0, concat_axis=0, tiled=True)

    vmem = pl.BlockSpec(memory_space=pltpu.VMEM)
    smem = pl.BlockSpec(memory_space=pltpu.SMEM)
    value_tiles = values.reshape(rows, 8, width // 8)
    value_grad, product = call(
        functools.partial(serve_kernel, n, rows),
        (shape((rows, width), BF16), shape((devices, LANES), F32)),
        limit=60,
        grid=(devices // GROUP,),
        in_specs=[
            smem,
            smem,
            pl.BlockSpec((GROUP * n, 8, width // 8), lambda i: (i, 0, 0)),
            vmem,
        ],
        out_specs=[vmem, vmem],
        scratch_shapes=[pltpu.VMEM((rows * 8, LANES), F32), pltpu.VMEM((CAP * 8, LANES), F32)],
    )(slot_index.reshape(devices, LANES), slot_weight.reshape(devices, LANES), all_grad, value_tiles)
    returned = lax.all_to_all(product.reshape(devices, 1, LANES), ALL, split_axis=0, concat_axis=0, tiled=True)

    query_grad, key_grad, sums = call(
        functools.partial(back_kernel, heads, top, half),
        (shape((n, width), F32), shape((2, heads, subkeys, half), F32), shape((2, width), F32)),
    )(
        returned.reshape(devices, LANES), shard_ids, second_ids, pos, dense, weight, query, normed,
        first_split, second_keys,
    )
    shift_grad, gain_grad = all_sum(sums)
    raw_grad = (
        gain * inverse * (query_grad - shift_grad / everything - normed * gain_grad / everything)
    ).astype(BF16)
    token_grad = lax.dot_general(raw_grad, query_weight, NT, preferred_element_type=F32).astype(BF16)
    weight_part = lax.dot_general(raw_grad, tokens, TN, preferred_element_type=F32)
    query_weight_grad = scatter_sum(weight_part.reshape(devices // 2, 2, width // devices, width), BF16)

    blocks = key_grad.reshape(devices // 2, 2, -1, half)
    own_keys = scatter_sum(blocks, BF16)
    chip_keys = everyone(own_keys, CHIPS)
    other_keys = swap_core(chip_keys)
    core = lax.axis_index("c")
    key_grad = jnp.where(
        core == 0, jnp.stack([chip_keys, other_keys], 1), jnp.stack([other_keys, chip_keys], 1)
    ).reshape(2, heads, subkeys, half)
    first_key_grad = key_grad[0].reshape(heads, subkeys // devices, devices, half).swapaxes(1, 2)
    return (
        token_grad,
        query_weight_grad,
        gain_grad,
        shift_grad,
        first_key_grad.reshape(heads, subkeys, half),
        key_grad[1],
        value_grad.reshape(heads, rows_dev, width),
    )


def solution(mesh):
    fine = Mesh(mesh.devices.reshape(4, 4, 4, 2), ALL)
    split_rows = P(ALL, None)
    in_specs = (
        split_rows, split_rows, P(), P(), P(), P(), P(), P(None, ALL, None),
        P(ALL, None, None), P(ALL, None, None), P(ALL, None, None),
    )
    out_specs = (split_rows, split_rows, P(), P(), P(), P(), P(None, ALL, None))
    return jax.shard_map(per_device, mesh=fine, in_specs=in_specs, out_specs=out_specs, check_vma=False)
```

```python
import functools
import jax
import jax.numpy as jnp
from jax import lax
from jax.experimental import pallas as pl
from jax.experimental.pallas import tpu as pltpu
from jax.sharding import Mesh, PartitionSpec as P

epsilon = 1e-05
F32, BF16, I32 = jnp.float32, jnp.bfloat16, jnp.int32
ALL = ("x", "z", "y", "c")
CHIPS = ("x", "z", "y")
CAP = 40
GROUP = 8
LANES = 128
NT = (((1,), (1,)), ((), ()))
TN = (((0,), (0,)), ((), ()))


def iota(shape, axis):
    return lax.broadcasted_iota(I32, shape, axis)


def slot_table(pos, payload):
    lines = []
    for j in range(CAP):
        found = sum(jnp.where(p == j, v, jnp.zeros_like(v)) for p, v in zip(pos, payload))
        lines.append(jnp.sum(found, axis=0, keepdims=True))
    lines.append(jnp.zeros((LANES - CAP, LANES), payload[0].dtype))
    return lines


def slots_kernel(heads, top, shard_ref, code_ref, pos_ref, dense_ref, slot_ref):
    n = shard_ref.shape[0]
    lane = iota((n, LANES), 1)
    row = iota((n, LANES), 0)
    below = (iota((n, n), 1) < iota((n, n), 0)).astype(BF16)
    before = jnp.zeros((1, LANES), F32)
    pos, packed = [], []
    for h in range(heads):
        code = jnp.full((n, LANES), -1, I32)
        for k in range(top):
            at = h * top + k
            code = jnp.where(shard_ref[:, at : at + 1] == lane, code_ref[:, at : at + 1], code)
        hit = code >= 0
        ones = jnp.where(hit, 1.0, 0.0)
        place = jnp.dot(below, ones.astype(BF16), preferred_element_type=F32) + before
        before = before + jnp.sum(ones, axis=0, keepdims=True)
        place = jnp.where(hit, place, -1.0)
        pos.append(place)
        packed.append(((h * 2048 + code) * n + row + 1).astype(F32))
        pos_ref[h * n : (h + 1) * n, :] = place
        dense_ref[h * n : (h + 1) * n, :] = code
    table = jnp.concatenate(slot_table(pos, packed)[:CAP], axis=0).astype(I32) - 1
    table = jnp.where(table < 0, (heads * 2048 + iota((CAP, LANES), 0)) * n, table)
    clash = jnp.zeros((8, LANES), I32)
    for b in range(CAP // 8):
        target = table[b * 8 : b * 8 + 8, :] >> 7
        for d in range(1, 5):
            clash = jnp.where(pltpu.roll(target, d, 0) == target, 1, clash)
    clash = jnp.max(clash.astype(F32), axis=0, keepdims=True)
    rest = jnp.zeros((LANES - CAP - 1, LANES), F32)
    slot_ref[...] = jnp.concatenate([table.astype(F32), clash, rest], axis=0).T.astype(I32)


def score_kernel(
    heads, half, raw_ref, stat_ref, gain_ref, shift_ref, first_ref, second_ref, pos_ref, dense_ref,
    query_ref, normed_ref, weight_ref, slot_ref,
):
    n = raw_ref.shape[0]
    normed = (raw_ref[...] - stat_ref[0:1, :]) * stat_ref[1:2, :]
    normed_ref[...] = normed
    query = (normed * gain_ref[...] + shift_ref[...]).astype(BF16)
    query_ref[...] = query
    pos, weights = [], []
    for h in range(heads):
        code = dense_ref[h * n : (h + 1) * n, :]
        hit = code >= 0
        low = code >> 9
        second = jnp.maximum(code, 0) & 511
        base = h * 2 * half
        near = query[:, base : base + half]
        far = query[:, base + half : base + 2 * half]
        score = jnp.zeros((n, LANES), F32)
        for part in range(4):
            dense = lax.dot_general(
                near, first_ref[h, part * LANES : (part + 1) * LANES, :], NT, preferred_element_type=F32
            )
            score = jnp.where(low == part, dense, score)
        found = jnp.zeros((n, LANES), F32)
        for part in range(4):
            dense = lax.dot_general(
                far, second_ref[h, part * LANES : (part + 1) * LANES, :], NT, preferred_element_type=F32
            )
            taken = jnp.take_along_axis(dense, second & (LANES - 1), axis=1)
            found = jnp.where((second >> 7) == part, taken, found)
        score = jnp.where(hit, score + found, -jnp.inf)
        most = jnp.max(score, axis=1, keepdims=True)
        power = jnp.where(hit, jnp.exp(score - most), 0.0)
        weight = power / jnp.sum(power, axis=1, keepdims=True)
        weight_ref[h * n : (h + 1) * n, :] = weight
        pos.append(pos_ref[h * n : (h + 1) * n, :])
        weights.append(weight)
    slot_ref[...] = jnp.concatenate(slot_table(pos, weights), axis=0).T


def slot_of(index_ref, weight_ref, grad_ref, sender, g, j, tokens):
    packed = index_ref[sender, j]
    grad = grad_ref[g * tokens + (packed & (tokens - 1))].astype(F32)
    message = (grad * weight_ref[sender, j]).astype(BF16).astype(F32)
    return packed >> 7, message


def product_kernel(tokens, rows, index_ref, weight_ref, grad_ref, value_ref, product_ref, held):
    step = pl.program_id(0)
    eye = iota((CAP, LANES), 0) == iota((CAP, LANES), 1)

    def one_sender(g, carry):
        for j in range(CAP):
            row, message = slot_of(index_ref, weight_ref, grad_ref, step * GROUP + g, g, j, tokens)
            value = value_ref[row & (rows - 1)].astype(F32)
            held[pl.ds(pl.multiple_of((g * CAP + j) * 8, 8), 8), :] = message * value
        return carry

    lax.fori_loop(0, GROUP, one_sender, 0)
    for g in range(GROUP):
        part = held[pl.ds(g * CAP * 8, CAP, stride=8), :]
        for c in range(1, 8):
            part = part + held[pl.ds(g * CAP * 8 + c, CAP, stride=8), :]
        summed = jnp.sum(part, axis=1, keepdims=True)
        product_ref[g : g + 1, :] = jnp.sum(jnp.where(eye, summed, 0.0), axis=0, keepdims=True)


def spot(row):
    return pl.ds(pl.multiple_of(row * 8, 8), 8)


def add_messages(tokens, first, index_ref, weight_ref, grad_ref, total):
    def one_sender(g, carry):
        sender = first + g
        clash = index_ref[sender, CAP]

        @pl.when(clash == 0)
        def _():
            for b in range(CAP // 8):
                slots = [
                    slot_of(index_ref, weight_ref, grad_ref, sender, g, b * 8 + u, tokens) for u in range(8)
                ]
                sums = [total[spot(row), :] + message for row, message in slots]
                for (row, _), value in zip(slots, sums):
                    total[spot(row), :] = value

        @pl.when(clash != 0)
        def _():
            def one(j, inner):
                row, message = slot_of(index_ref, weight_ref, grad_ref, sender, g, j, tokens)
                total[spot(row), :] += message
                return inner

            lax.fori_loop(0, CAP, one, 0)

        return carry

    lax.fori_loop(0, GROUP, one_sender, 0)


def clear_all(total):
    def clear(i, carry):
        at = pl.multiple_of(i * 352, 8)
        total[pl.ds(at, 352), :] = jnp.zeros((352, LANES), F32)
        return carry

    lax.fori_loop(0, total.shape[0] // 352, clear, 0)


def early_kernel(tokens, index_ref, weight_ref, grad_ref, after_ref, total, done_ref):
    step = pl.program_id(0)
    done_ref[...] = jnp.zeros((8, LANES), F32)

    @pl.when(step == 0)
    def _():
        clear_all(total)

    add_messages(tokens, step * GROUP, index_ref, weight_ref, grad_ref, total)


def late_kernel(
    tokens, senders, index_ref, weight_ref, grad_ref, early_ref, after_ref, out_ref, done_ref, total, sem
):
    step = pl.program_id(0)
    done_ref[...] = jnp.zeros((8, LANES), F32)

    @pl.when(step == 0)
    def _():
        copy = pltpu.make_async_copy(early_ref, total, sem)
        copy.start()
        copy.wait()

    add_messages(tokens, senders + step * GROUP, index_ref, weight_ref, grad_ref, total)

    @pl.when(step == pl.num_programs(0) - 1)
    def _():
        def emit(i, carry):
            for u in range(4):
                at = pl.multiple_of(i * 64 + u * 16, 16)
                for c in range(8):
                    out_ref[pl.ds(at, 16), c * LANES : (c + 1) * LANES] = total[
                        pl.ds(at * 8 + c, 16, stride=8), :
                    ].astype(BF16)
            return carry

        lax.fori_loop(0, out_ref.shape[0] // 64, emit, 0)


def split(value):
    high = value.astype(BF16)
    return high, (value - high.astype(F32)).astype(BF16)


def back_kernel(
    heads, top, half, back_ref, shard_ref, second_ids_ref, pos_ref, dense_ref, weight_ref, query_ref,
    normed_ref, first_ref, second_ref, core_ref, grad_ref, own_ref, other_ref, sum_ref, held,
):
    n = query_ref.shape[0]
    core = core_ref[0]
    table = back_ref[...].T
    wide = iota((n, 4 * LANES), 1)
    for h in range(heads):
        pos = pos_ref[h * n : (h + 1) * n, :]
        product = jnp.zeros((n, LANES), F32)
        for j in range(CAP):
            product = jnp.where(pos == j, table[j : j + 1, :], product)
        weight = weight_ref[h * n : (h + 1) * n, :]
        score = product - weight * jnp.sum(product, axis=1, keepdims=True)
        code = dense_ref[h * n : (h + 1) * n, :]
        low = code >> 9
        near_dense = jnp.concatenate([jnp.where(low == part, score, 0.0) for part in range(4)], axis=1)
        shards = jnp.concatenate(
            [shard_ref[:, h * top : (h + 1) * top], jnp.zeros((n, LANES - top), I32)], axis=1
        )
        picked = jnp.take_along_axis(score, shards, axis=1)
        far_dense = jnp.zeros((n, 4 * LANES), F32)
        for k in range(top):
            at = h * top + k
            far_dense = far_dense + jnp.where(
                second_ids_ref[:, at : at + 1] == wide, picked[:, k : k + 1], 0.0
            )
        base = h * 2 * half
        for side, dense, keys in ((0, near_dense, first_ref), (1, far_dense, second_ref)):
            cols = slice(base + side * half, base + (side + 1) * half)
            high, rest = split(dense)
            table_h = keys[h]
            grad = jnp.dot(high, table_h, preferred_element_type=F32) + jnp.dot(
                rest, table_h, preferred_element_type=F32
            )
            grad_ref[:, cols] = grad
            at = h * 2 + side
            sum_ref[at : at + 1, :] = jnp.sum(grad, axis=0, keepdims=True)
            sum_ref[at + 4 : at + 5, :] = jnp.sum(grad * normed_ref[:, cols], axis=0, keepdims=True)
            query = query_ref[:, cols]
            keys_grad = lax.dot_general(high, query, TN, preferred_element_type=F32) + lax.dot_general(
                rest, query, TN, preferred_element_type=F32
            )
            blocks = keys_grad.reshape(16, 2, 2, 8, half)
            first = (side * heads + h) * 16
            held[first : first + 16, :, :, 0:half] = blocks[:, :, 0]
            held[first : first + 16, :, :, half : 2 * half] = blocks[:, :, 1]
    own_ref[...] = held[:, core]
    other_ref[...] = held[:, 1 - core]


def tail_kernel(
    everything, arrived_ref, query_grad_ref, normed_ref, gain_ref, stat_ref, tokens_ref, core_ref, after_ref,
    raw_ref, own_ref, other_ref, sum_ref, block_ref, held,
):
    core = core_ref[0]
    half = 256
    reduced = jnp.sum(arrived_ref[...], axis=0)
    block_ref[...] = reduced[:, half:].astype(BF16)
    shift_sum = jnp.concatenate([reduced[i : i + 1, :half] for i in range(4)], axis=1)
    gain_sum = jnp.concatenate([reduced[i : i + 1, :half] for i in range(4, 8)], axis=1)
    sum_ref[0:1, :] = shift_sum
    sum_ref[1:2, :] = gain_sum
    raw_grad = (
        gain_ref[...]
        * stat_ref[1:2, :]
        * (query_grad_ref[...] - shift_sum / everything - normed_ref[...] * gain_sum / everything)
    ).astype(BF16)
    raw_ref[...] = raw_grad
    part = lax.dot_general(raw_grad, tokens_ref[...], TN, preferred_element_type=F32)
    held[...] = part.reshape(held.shape)
    own_ref[...] = held[:, core]
    other_ref[...] = held[:, 1 - core]


def sum_kernel(arrived_ref, after_ref, sum_ref, mine_ref):
    width = sum_ref.shape[1]
    sum_ref[...] = jnp.sum(arrived_ref[:, :, :width].astype(F32), axis=0)
    mine_ref[...] = arrived_ref[:, :, width:]


def keys_kernel(heads, mine_ref, theirs_ref, core_ref, first_ref, second_ref, held):
    subkeys, half = first_ref.shape[1:]
    at_zero = core_ref[0] == 0
    each = subkeys // 32
    source = iota((subkeys, subkeys), 0)
    source = (source & 3) * LANES + (source >> 2)
    order = (iota((subkeys, subkeys), 1) == source).astype(BF16)
    for side in range(2):
        for h in range(heads):
            at = (side * heads + h) * each
            mine = mine_ref[at : at + each].astype(F32)
            theirs = theirs_ref[at : at + each].astype(F32)
            pair = (jnp.where(at_zero, mine, theirs), jnp.where(at_zero, theirs, mine))
            for c in range(2):
                held[:, c, 0] = pair[c][:, :, :half]
                held[:, c, 1] = pair[c][:, :, half:]
            keys = held[...].reshape(subkeys, half)
            if side == 0:
                first_ref[h] = jnp.dot(order, keys.astype(BF16), preferred_element_type=F32)
            else:
                second_ref[h] = keys


def call(kernel, out_shape, limit=16, **more):
    return pl.pallas_call(
        kernel,
        out_shape=out_shape,
        compiler_params=pltpu.CompilerParams(vmem_limit_bytes=limit << 20),
        **more,
    )


def shape(dims, dtype):
    return jax.ShapeDtypeStruct(dims, dtype)


def swap_core(value):
    return lax.ppermute(value, "c", [(0, 1), (1, 0)])


def everyone(value, axis):
    size = lax.axis_size(axis)
    wide = jnp.broadcast_to(value[None], (size,) + value.shape)
    return lax.all_to_all(wide, axis, split_axis=0, concat_axis=0, tiled=True)


def all_moments(mean, spread, count):
    for axis in ("c", "y", "z", "x"):
        both = jnp.stack([mean, spread])
        parts = jnp.stack([both, swap_core(both)]) if axis == "c" else everyone(both, axis)
        mean = jnp.mean(parts[:, 0], axis=0)
        spread = jnp.sum(parts[:, 1] + count * jnp.square(parts[:, 0] - mean), axis=0)
        count = count * parts.shape[0]
    return mean, spread / count


def exchange(value, axis):
    return lax.all_to_all(value, axis, split_axis=0, concat_axis=0, tiled=True)


def per_device(
    tokens, out_grad, query_weight, gain, shift, first_keys, second_keys, values, pick_shard, pick_low,
    pick_second,
):
    devices = lax.axis_size(ALL)
    n = tokens.shape[0]
    heads, rows_dev, width = values.shape
    subkeys, half = first_keys.shape[1:]
    top = pick_shard.shape[2]
    everything = n * devices
    rows = heads * rows_dev

    tiles = out_grad.reshape(n, 8, width // 8)
    all_grad = lax.all_gather(tiles, ALL, axis=0, tiled=True)

    raw_query = jnp.dot(tokens, query_weight, preferred_element_type=F32)
    local_mean = jnp.mean(raw_query, axis=0)
    local_spread = jnp.sum(jnp.square(raw_query - local_mean), axis=0)
    centre, spread = all_moments(local_mean, local_spread, n)
    inverse = 1.0 / jnp.sqrt(spread + epsilon)

    stats = jnp.stack([centre, inverse])
    shard_ids = pick_shard.reshape(n, heads * top)
    second_ids = pick_second.reshape(n, heads * top)
    code = pick_low.reshape(n, heads * top) * subkeys + second_ids
    pos, dense, slot_index = call(
        functools.partial(slots_kernel, heads, top),
        (shape((heads * n, LANES), F32), shape((heads * n, LANES), I32), shape((devices, LANES), I32)),
    )(shard_ids, code)
    slot_index = lax.all_to_all(slot_index.reshape(devices, 1, LANES), ALL, split_axis=0, concat_axis=0, tiled=True)

    first_split = first_keys.reshape(heads, devices, subkeys // devices, half).swapaxes(1, 2)
    first_split = first_split.reshape(heads, subkeys, half)
    query, normed, weight, slot_weight = call(
        functools.partial(score_kernel, heads, half),
        (
            shape((n, width), BF16),
            shape((n, width), F32),
            shape((heads * n, LANES), F32),
            shape((devices, LANES), F32),
        ),
    )(
        raw_query, stats, gain[None], shift[None], first_split, second_keys, pos, dense
    )
    slot_weight = lax.all_to_all(slot_weight.reshape(devices, 1, LANES), ALL, split_axis=0, concat_axis=0, tiled=True)

    vmem = pl.BlockSpec(memory_space=pltpu.VMEM)
    smem = pl.BlockSpec(memory_space=pltpu.SMEM)
    hbm = pl.BlockSpec(memory_space=pltpu.HBM)
    value_tiles = values.reshape(rows, 8, width // 8)
    index_table = slot_index.reshape(devices, LANES)
    weight_table = slot_weight.reshape(devices, LANES)
    grad_spec = pl.BlockSpec((GROUP * n, 8, width // 8), lambda i: (i, 0, 0))
    product = call(
        functools.partial(product_kernel, n, rows),
        shape((devices, LANES), F32),
        limit=28,
        grid=(devices // GROUP,),
        in_specs=[smem, smem, grad_spec, vmem],
        out_specs=pl.BlockSpec((GROUP, LANES), lambda i: (i, 0)),
        scratch_shapes=[pltpu.VMEM((GROUP * CAP * 8, LANES), F32)],
    )(index_table, weight_table, all_grad, value_tiles)
    returned = exchange(product.reshape(devices, 1, LANES), ALL)

    chips = devices // 2
    core = jnp.reshape(lax.axis_index("c"), (1,)).astype(I32)
    query_grad, own_keys, other_keys, sums = call(
        functools.partial(back_kernel, heads, top, half),
        (
            shape((n, width), F32),
            shape((chips, 8, 2 * half), F32),
            shape((chips, 8, 2 * half), F32),
            shape((8, half), F32),
        ),
        in_specs=[vmem] * 10 + [smem],
        scratch_shapes=[pltpu.VMEM((chips, 2, 8, 2 * half), F32)],
    )(
        returned.reshape(devices, LANES), shard_ids, second_ids, pos, dense, weight, query, normed,
        first_split, second_keys, core,
    )
    keys_in, sums_in = swap_core((other_keys, sums))
    sums = jnp.broadcast_to((sums + sums_in)[None], (chips, 8, half))
    sent = jnp.concatenate([sums, own_keys + keys_in], axis=2)
    arrived = exchange(sent, CHIPS)
    steps = devices // GROUP // 2
    early, early_done = call(
        functools.partial(early_kernel, n),
        (shape(((rows + CAP) * 8, LANES), F32), shape((8, LANES), F32)),
        limit=32,
        grid=(steps,),
        in_specs=[smem, smem, grad_spec, vmem],
        out_specs=[vmem, vmem],
    )(index_table, weight_table, all_grad, sent[0, :, :LANES])

    raw_grad, own_part, other_part, sums, key_block = call(
        functools.partial(tail_kernel, everything),
        (
            shape((n, width), BF16),
            shape((chips, 8, width), F32),
            shape((chips, 8, width), F32),
            shape((2, width), F32),
            shape((8, 2 * half), BF16),
        ),
        in_specs=[vmem] * 6 + [smem, vmem],
        scratch_shapes=[pltpu.VMEM((chips, 2, 8, width), F32)],
        limit=24,
    )(arrived, query_grad, normed, gain[None], stats, tokens, core, early_done)
    shift_grad, gain_grad = sums
    other_part = swap_core(other_part)
    own_part = (own_part + other_part).astype(BF16)
    key_wide = jnp.broadcast_to(key_block[None], (chips, 8, 2 * half))
    sent = jnp.concatenate([own_part, key_wide], axis=2)
    arrived = exchange(sent, CHIPS)
    token_grad = lax.dot_general(raw_grad, query_weight, NT, preferred_element_type=F32).astype(BF16)
    value_grad, late_done = call(
        functools.partial(late_kernel, n, steps * GROUP),
        (shape((rows, width), BF16), shape((8, LANES), F32)),
        limit=50,
        grid=(steps,),
        in_specs=[
            smem,
            smem,
            pl.BlockSpec((GROUP * n, 8, width // 8), lambda i: (i + steps, 0, 0)),
            hbm,
            vmem,
        ],
        out_specs=[vmem, vmem],
        scratch_shapes=[pltpu.VMEM(((rows + CAP) * 8, LANES), F32), pltpu.SemaphoreType.DMA],
    )(index_table, weight_table, all_grad, early, other_part[0, :, :LANES])

    query_weight_grad, mine = call(
        sum_kernel,
        (shape((8, width), F32), shape((chips, 8, 2 * half), BF16)),
        in_specs=[vmem, vmem],
        limit=16,
    )(arrived, late_done)
    first_key_grad, second_key_grad = call(
        functools.partial(keys_kernel, heads),
        (shape(first_keys.shape, F32), shape(second_keys.shape, F32)),
        in_specs=[vmem, vmem, smem],
        scratch_shapes=[pltpu.VMEM((chips // 4, 2, 2, 8, half), F32)],
        limit=16,
    )(mine, swap_core(mine), core)
    return (
        token_grad,
        query_weight_grad,
        gain_grad,
        shift_grad,
        first_key_grad,
        second_key_grad,
        value_grad.reshape(heads, rows_dev, width),
    )


def solution(mesh):
    fine = Mesh(mesh.devices.reshape(4, 4, 4, 2), ALL)
    split_rows = P(ALL, None)
    in_specs = (
        split_rows, split_rows, P(), P(), P(), P(), P(), P(None, ALL, None),
        P(ALL, None, None), P(ALL, None, None), P(ALL, None, None),
    )
    out_specs = (split_rows, split_rows, P(), P(), P(), P(), P(None, ALL, None))
    return jax.shard_map(per_device, mesh=fine, in_specs=in_specs, out_specs=out_specs, check_vma=False)
```

```python
import functools
import jax
import jax.numpy as jnp
from jax import lax
from jax.experimental import pallas as pl
from jax.experimental.pallas import tpu as pltpu
from jax.sharding import Mesh, PartitionSpec as P

epsilon = 1e-05
F32, BF16, I32 = jnp.float32, jnp.bfloat16, jnp.int32
ALL = ("x", "z", "y", "c")
CHIPS = ("x", "z", "y")
CAP = 40
GROUP = 8
BLOCK = 1024
LANES = 128
NT = (((1,), (1,)), ((), ()))
TN = (((0,), (0,)), ((), ()))


def iota(shape, axis):
    return lax.broadcasted_iota(I32, shape, axis)


def slot_table(pos, payload):
    lines = []
    for j in range(CAP):
        found = sum(jnp.where(p == j, v, jnp.zeros_like(v)) for p, v in zip(pos, payload))
        lines.append(jnp.sum(found, axis=0, keepdims=True))
    lines.append(jnp.zeros((LANES - CAP, LANES), payload[0].dtype))
    return lines


def slots_kernel(heads, top, shard_ref, code_ref, place_ref, pos_ref, dense_ref, slot_ref):
    n = shard_ref.shape[0]
    offset = place_ref[0]
    lane = iota((n, LANES), 1)
    row = iota((n, LANES), 0)
    below = (iota((n, n), 1) < iota((n, n), 0)).astype(BF16)
    before = jnp.zeros((1, LANES), F32)
    pos, packed = [], []
    for h in range(heads):
        code = jnp.full((n, LANES), -1, I32)
        for k in range(top):
            at = h * top + k
            code = jnp.where(shard_ref[:, at : at + 1] == lane, code_ref[:, at : at + 1], code)
        hit = code >= 0
        ones = jnp.where(hit, 1.0, 0.0)
        place = jnp.dot(below, ones.astype(BF16), preferred_element_type=F32) + before
        before = before + jnp.sum(ones, axis=0, keepdims=True)
        place = jnp.where(hit, place, -1.0)
        pos.append(place)
        packed.append(((h * 2048 + code) * BLOCK + offset + row + 1).astype(F32))
        pos_ref[h * n : (h + 1) * n, :] = place
        dense_ref[h * n : (h + 1) * n, :] = code
    table = jnp.concatenate(slot_table(pos, packed)[:CAP], axis=0).astype(I32) - 1
    table = jnp.where(table < 0, (heads * 2048 + iota((CAP, LANES), 0)) * BLOCK, table)
    clash = jnp.zeros((8, LANES), I32)
    for b in range(CAP // 8):
        target = table[b * 8 : b * 8 + 8, :] >> 10
        for d in range(1, 5):
            clash = jnp.where(pltpu.roll(target, d, 0) == target, 1, clash)
    clash = jnp.max(clash.astype(F32), axis=0, keepdims=True) * BLOCK
    rest = jnp.zeros((LANES - CAP - 1, LANES), F32)
    slot_ref[...] = jnp.concatenate([table.astype(F32), clash, rest], axis=0).T.astype(I32)


def score_kernel(
    heads, half, raw_ref, stat_ref, gain_ref, shift_ref, first_ref, second_ref, pos_ref, dense_ref,
    query_ref, normed_ref, weight_ref, slot_ref,
):
    n = raw_ref.shape[0]
    normed = (raw_ref[...] - stat_ref[0:1, :]) * stat_ref[1:2, :]
    normed_ref[...] = normed
    query = (normed * gain_ref[...] + shift_ref[...]).astype(BF16)
    query_ref[...] = query
    pos, weights = [], []
    for h in range(heads):
        code = dense_ref[h * n : (h + 1) * n, :]
        hit = code >= 0
        low = code >> 9
        second = jnp.maximum(code, 0) & 511
        base = h * 2 * half
        near = query[:, base : base + half]
        far = query[:, base + half : base + 2 * half]
        score = jnp.zeros((n, LANES), F32)
        for part in range(4):
            dense = lax.dot_general(
                near, first_ref[h, part * LANES : (part + 1) * LANES, :], NT, preferred_element_type=F32
            )
            score = jnp.where(low == part, dense, score)
        found = jnp.zeros((n, LANES), F32)
        for part in range(4):
            dense = lax.dot_general(
                far, second_ref[h, part * LANES : (part + 1) * LANES, :], NT, preferred_element_type=F32
            )
            taken = jnp.take_along_axis(dense, second & (LANES - 1), axis=1)
            found = jnp.where((second >> 7) == part, taken, found)
        score = jnp.where(hit, score + found, -jnp.inf)
        most = jnp.max(score, axis=1, keepdims=True)
        power = jnp.where(hit, jnp.exp(score - most), 0.0)
        weight = power / jnp.sum(power, axis=1, keepdims=True)
        weight_ref[h * n : (h + 1) * n, :] = weight
        pos.append(pos_ref[h * n : (h + 1) * n, :])
        weights.append(weight)
    slot_ref[...] = jnp.concatenate(slot_table(pos, weights), axis=0).T


def slot_of(row_ref, token_ref, weight_ref, grad_ref, sender, j):
    grad = grad_ref[token_ref[sender, j]].astype(F32)
    message = (grad * weight_ref[sender, j]).astype(BF16).astype(F32)
    return row_ref[sender, j], message


def product_kernel(row_ref, token_ref, weight_ref, grad_ref, value_ref, product_ref, held):
    step = pl.program_id(0)
    eye = iota((CAP, LANES), 0) == iota((CAP, LANES), 1)

    def one_sender(g, carry):
        for j in range(CAP):
            row, message = slot_of(row_ref, token_ref, weight_ref, grad_ref, step * GROUP + g, j)
            value = value_ref[row].astype(F32)
            held[pl.ds(pl.multiple_of((g * CAP + j) * 8, 8), 8), :] = message * value
        return carry

    lax.fori_loop(0, GROUP, one_sender, 0)
    for g in range(GROUP):
        part = held[pl.ds(g * CAP * 8, CAP, stride=8), :]
        for c in range(1, 8):
            part = part + held[pl.ds(g * CAP * 8 + c, CAP, stride=8), :]
        summed = jnp.sum(part, axis=1, keepdims=True)
        product_ref[g : g + 1, :] = jnp.sum(jnp.where(eye, summed, 0.0), axis=0, keepdims=True)


def spot(row):
    return pl.ds(pl.multiple_of(row * 8, 8), 8)


def add_messages(first, row_ref, token_ref, weight_ref, grad_ref, total):
    def one_sender(g, carry):
        sender = first + g
        clash = row_ref[sender, CAP]

        @pl.when(clash == 0)
        def _():
            for b in range(CAP // 8):
                slots = [
                    slot_of(row_ref, token_ref, weight_ref, grad_ref, sender, b * 8 + u) for u in range(8)
                ]
                sums = [total[spot(row), :] + message for row, message in slots]
                for (row, _), value in zip(slots, sums):
                    total[spot(row), :] = value

        @pl.when(clash != 0)
        def _():
            def one(j, inner):
                row, message = slot_of(row_ref, token_ref, weight_ref, grad_ref, sender, j)
                total[spot(row), :] += message
                return inner

            lax.fori_loop(0, CAP, one, 0)

        return carry

    lax.fori_loop(0, GROUP, one_sender, 0)


def clear_all(total):
    def clear(i, carry):
        at = pl.multiple_of(i * 352, 8)
        total[pl.ds(at, 352), :] = jnp.zeros((352, LANES), F32)
        return carry

    lax.fori_loop(0, total.shape[0] // 352, clear, 0)


def early_kernel(row_ref, token_ref, weight_ref, grad_ref, after_ref, total, done_ref):
    step = pl.program_id(0)
    done_ref[...] = jnp.zeros((8, LANES), F32)

    @pl.when(step == 0)
    def _():
        clear_all(total)

    add_messages(step * GROUP, row_ref, token_ref, weight_ref, grad_ref, total)


def late_kernel(
    senders, row_ref, token_ref, weight_ref, grad_ref, early_ref, after_ref, out_ref, done_ref, total, sem
):
    step = pl.program_id(0)
    done_ref[...] = jnp.zeros((8, LANES), F32)

    @pl.when(step == 0)
    def _():
        copy = pltpu.make_async_copy(early_ref, total, sem)
        copy.start()
        copy.wait()

    add_messages(senders + step * GROUP, row_ref, token_ref, weight_ref, grad_ref, total)

    @pl.when(step == pl.num_programs(0) - 1)
    def _():
        def emit(i, carry):
            for u in range(4):
                at = pl.multiple_of(i * 64 + u * 16, 16)
                for c in range(8):
                    out_ref[pl.ds(at, 16), c * LANES : (c + 1) * LANES] = total[
                        pl.ds(at * 8 + c, 16, stride=8), :
                    ].astype(BF16)
            return carry

        lax.fori_loop(0, out_ref.shape[0] // 64, emit, 0)


def split(value):
    high = value.astype(BF16)
    return high, (value - high.astype(F32)).astype(BF16)


def back_kernel(
    heads, top, half, back_ref, shard_ref, second_ids_ref, pos_ref, dense_ref, weight_ref, query_ref,
    normed_ref, first_ref, second_ref, core_ref, grad_ref, own_ref, other_ref, sum_ref, held,
):
    n = query_ref.shape[0]
    core = core_ref[0]
    table = back_ref[...].T
    wide = iota((n, 4 * LANES), 1)
    for h in range(heads):
        pos = pos_ref[h * n : (h + 1) * n, :]
        product = jnp.zeros((n, LANES), F32)
        for j in range(CAP):
            product = jnp.where(pos == j, table[j : j + 1, :], product)
        weight = weight_ref[h * n : (h + 1) * n, :]
        score = product - weight * jnp.sum(product, axis=1, keepdims=True)
        code = dense_ref[h * n : (h + 1) * n, :]
        low = code >> 9
        near_dense = jnp.concatenate([jnp.where(low == part, score, 0.0) for part in range(4)], axis=1)
        shards = jnp.concatenate(
            [shard_ref[:, h * top : (h + 1) * top], jnp.zeros((n, LANES - top), I32)], axis=1
        )
        picked = jnp.take_along_axis(score, shards, axis=1)
        far_dense = jnp.zeros((n, 4 * LANES), F32)
        for k in range(top):
            at = h * top + k
            far_dense = far_dense + jnp.where(
                second_ids_ref[:, at : at + 1] == wide, picked[:, k : k + 1], 0.0
            )
        base = h * 2 * half
        for side, dense, keys in ((0, near_dense, first_ref), (1, far_dense, second_ref)):
            cols = slice(base + side * half, base + (side + 1) * half)
            high, rest = split(dense)
            table_h = keys[h]
            grad = jnp.dot(high, table_h, preferred_element_type=F32) + jnp.dot(
                rest, table_h, preferred_element_type=F32
            )
            grad_ref[:, cols] = grad
            at = h * 2 + side
            sum_ref[at : at + 1, :] = jnp.sum(grad, axis=0, keepdims=True)
            sum_ref[at + 4 : at + 5, :] = jnp.sum(grad * normed_ref[:, cols], axis=0, keepdims=True)
            query = query_ref[:, cols]
            keys_grad = lax.dot_general(high, query, TN, preferred_element_type=F32) + lax.dot_general(
                rest, query, TN, preferred_element_type=F32
            )
            blocks = keys_grad.reshape(16, 2, 2, 8, half)
            first = (side * heads + h) * 16
            held[first : first + 16, :, :, 0:half] = blocks[:, :, 0]
            held[first : first + 16, :, :, half : 2 * half] = blocks[:, :, 1]
    own_ref[...] = held[:, core]
    other_ref[...] = held[:, 1 - core]


def tail_kernel(
    everything, arrived_ref, query_grad_ref, normed_ref, gain_ref, stat_ref, tokens_ref, core_ref, after_ref,
    raw_ref, own_ref, other_ref, sum_ref, block_ref, held,
):
    core = core_ref[0]
    half = 256
    reduced = jnp.sum(arrived_ref[...], axis=0)
    block_ref[...] = reduced[:, half:].astype(BF16)
    shift_sum = jnp.concatenate([reduced[i : i + 1, :half] for i in range(4)], axis=1)
    gain_sum = jnp.concatenate([reduced[i : i + 1, :half] for i in range(4, 8)], axis=1)
    sum_ref[0:1, :] = shift_sum
    sum_ref[1:2, :] = gain_sum
    raw_grad = (
        gain_ref[...]
        * stat_ref[1:2, :]
        * (query_grad_ref[...] - shift_sum / everything - normed_ref[...] * gain_sum / everything)
    ).astype(BF16)
    raw_ref[...] = raw_grad
    part = lax.dot_general(raw_grad, tokens_ref[...], TN, preferred_element_type=F32)
    held[...] = part.reshape(held.shape)
    own_ref[...] = held[:, core]
    other_ref[...] = held[:, 1 - core]


def sum_kernel(arrived_ref, after_ref, sum_ref, mine_ref):
    width = sum_ref.shape[1]
    sum_ref[...] = jnp.sum(arrived_ref[:, :, :width].astype(F32), axis=0)
    mine_ref[...] = arrived_ref[:, :, width:]


def keys_kernel(heads, mine_ref, theirs_ref, core_ref, first_ref, second_ref, held):
    subkeys, half = first_ref.shape[1:]
    at_zero = core_ref[0] == 0
    each = subkeys // 32
    source = iota((subkeys, subkeys), 0)
    source = (source & 3) * LANES + (source >> 2)
    order = (iota((subkeys, subkeys), 1) == source).astype(BF16)
    for side in range(2):
        for h in range(heads):
            at = (side * heads + h) * each
            mine = mine_ref[at : at + each].astype(F32)
            theirs = theirs_ref[at : at + each].astype(F32)
            pair = (jnp.where(at_zero, mine, theirs), jnp.where(at_zero, theirs, mine))
            for c in range(2):
                held[:, c, 0] = pair[c][:, :, :half]
                held[:, c, 1] = pair[c][:, :, half:]
            keys = held[...].reshape(subkeys, half)
            if side == 0:
                first_ref[h] = jnp.dot(order, keys.astype(BF16), preferred_element_type=F32)
            else:
                second_ref[h] = keys


def call(kernel, out_shape, limit=16, **more):
    return pl.pallas_call(
        kernel,
        out_shape=out_shape,
        compiler_params=pltpu.CompilerParams(vmem_limit_bytes=limit << 20),
        **more,
    )


def shape(dims, dtype):
    return jax.ShapeDtypeStruct(dims, dtype)


def swap_core(value):
    return lax.ppermute(value, "c", [(0, 1), (1, 0)])


def everyone(value, axis):
    size = lax.axis_size(axis)
    wide = jnp.broadcast_to(value[None], (size,) + value.shape)
    return lax.all_to_all(wide, axis, split_axis=0, concat_axis=0, tiled=True)


def all_moments(mean, spread, count):
    for axis in ("c", "y", "z", "x"):
        both = jnp.stack([mean, spread])
        parts = jnp.stack([both, swap_core(both)]) if axis == "c" else everyone(both, axis)
        mean = jnp.mean(parts[:, 0], axis=0)
        spread = jnp.sum(parts[:, 1] + count * jnp.square(parts[:, 0] - mean), axis=0)
        count = count * parts.shape[0]
    return mean, spread / count


def exchange(value, axis):
    return lax.all_to_all(value, axis, split_axis=0, concat_axis=0, tiled=True)


def per_device(
    tokens, out_grad, query_weight, gain, shift, first_keys, second_keys, values, pick_shard, pick_low,
    pick_second,
):
    devices = lax.axis_size(ALL)
    n = tokens.shape[0]
    heads, rows_dev, width = values.shape
    subkeys, half = first_keys.shape[1:]
    top = pick_shard.shape[2]
    everything = n * devices
    rows = heads * rows_dev

    tiles = out_grad.reshape(n, 8, width // 8)
    all_grad = lax.all_gather(tiles, ALL, axis=0, tiled=True)

    raw_query = jnp.dot(tokens, query_weight, preferred_element_type=F32)
    local_mean = jnp.mean(raw_query, axis=0)
    local_spread = jnp.sum(jnp.square(raw_query - local_mean), axis=0)
    centre, spread = all_moments(local_mean, local_spread, n)
    inverse = 1.0 / jnp.sqrt(spread + epsilon)

    stats = jnp.stack([centre, inverse])
    shard_ids = pick_shard.reshape(n, heads * top)
    second_ids = pick_second.reshape(n, heads * top)
    code = pick_low.reshape(n, heads * top) * subkeys + second_ids
    vmem = pl.BlockSpec(memory_space=pltpu.VMEM)
    smem = pl.BlockSpec(memory_space=pltpu.SMEM)
    hbm = pl.BlockSpec(memory_space=pltpu.HBM)
    place = jnp.reshape(lax.axis_index(ALL) % GROUP * n, (1,)).astype(I32)
    pos, dense, slot_index = call(
        functools.partial(slots_kernel, heads, top),
        (shape((heads * n, LANES), F32), shape((heads * n, LANES), I32), shape((devices, LANES), I32)),
        in_specs=[vmem, vmem, smem],
    )(shard_ids, code, place)
    slot_index = lax.all_to_all(slot_index.reshape(devices, 1, LANES), ALL, split_axis=0, concat_axis=0, tiled=True)

    first_split = first_keys.reshape(heads, devices, subkeys // devices, half).swapaxes(1, 2)
    first_split = first_split.reshape(heads, subkeys, half)
    query, normed, weight, slot_weight = call(
        functools.partial(score_kernel, heads, half),
        (
            shape((n, width), BF16),
            shape((n, width), F32),
            shape((heads * n, LANES), F32),
            shape((devices, LANES), F32),
        ),
    )(
        raw_query, stats, gain[None], shift[None], first_split, second_keys, pos, dense
    )
    slot_weight = lax.all_to_all(slot_weight.reshape(devices, 1, LANES), ALL, split_axis=0, concat_axis=0, tiled=True)

    value_tiles = values.reshape(rows, 8, width // 8)
    slot_index = slot_index.reshape(devices, LANES)
    row_table = slot_index >> 10
    token_table = slot_index & (BLOCK - 1)
    weight_table = slot_weight.reshape(devices, LANES)
    grad_spec = pl.BlockSpec((GROUP * n, 8, width // 8), lambda i: (i, 0, 0))
    product = call(
        product_kernel,
        shape((devices, LANES), F32),
        limit=28,
        grid=(devices // GROUP,),
        in_specs=[smem, smem, smem, grad_spec, vmem],
        out_specs=pl.BlockSpec((GROUP, LANES), lambda i: (i, 0)),
        scratch_shapes=[pltpu.VMEM((GROUP * CAP * 8, LANES), F32)],
    )(row_table & (rows - 1), token_table, weight_table, all_grad, value_tiles)
    returned = exchange(product.reshape(devices, 1, LANES), ALL)

    chips = devices // 2
    core = jnp.reshape(lax.axis_index("c"), (1,)).astype(I32)
    query_grad, own_keys, other_keys, sums = call(
        functools.partial(back_kernel, heads, top, half),
        (
            shape((n, width), F32),
            shape((chips, 8, 2 * half), F32),
            shape((chips, 8, 2 * half), F32),
            shape((8, half), F32),
        ),
        in_specs=[vmem] * 10 + [smem],
        scratch_shapes=[pltpu.VMEM((chips, 2, 8, 2 * half), F32)],
    )(
        returned.reshape(devices, LANES), shard_ids, second_ids, pos, dense, weight, query, normed,
        first_split, second_keys, core,
    )
    keys_in, sums_in = swap_core((other_keys, sums))
    sums = jnp.broadcast_to((sums + sums_in)[None], (chips, 8, half))
    sent = jnp.concatenate([sums, own_keys + keys_in], axis=2)
    arrived = exchange(sent, CHIPS)
    steps = 10
    rest = devices // GROUP - steps
    early, early_done = call(
        early_kernel,
        (shape(((rows + CAP) * 8, LANES), F32), shape((8, LANES), F32)),
        limit=32,
        grid=(steps,),
        in_specs=[smem, smem, smem, grad_spec, vmem],
        out_specs=[vmem, vmem],
    )(row_table, token_table, weight_table, all_grad, sent[0, :, :LANES])

    raw_grad, own_part, other_part, sums, key_block = call(
        functools.partial(tail_kernel, everything),
        (
            shape((n, width), BF16),
            shape((chips, 8, width), F32),
            shape((chips, 8, width), F32),
            shape((2, width), F32),
            shape((8, 2 * half), BF16),
        ),
        in_specs=[vmem] * 6 + [smem, vmem],
        scratch_shapes=[pltpu.VMEM((chips, 2, 8, width), F32)],
        limit=24,
    )(arrived, query_grad, normed, gain[None], stats, tokens, core, early_done)
    shift_grad, gain_grad = sums
    other_part = swap_core(other_part)
    own_part = (own_part + other_part).astype(BF16)
    key_wide = jnp.broadcast_to(key_block[None], (chips, 8, 2 * half))
    sent = jnp.concatenate([own_part, key_wide], axis=2)
    arrived = exchange(sent, CHIPS)
    token_grad = lax.dot_general(raw_grad, query_weight, NT, preferred_element_type=F32).astype(BF16)
    value_grad, late_done = call(
        functools.partial(late_kernel, steps * GROUP),
        (shape((rows, width), BF16), shape((8, LANES), F32)),
        limit=50,
        grid=(rest,),
        in_specs=[
            smem,
            smem,
            smem,
            pl.BlockSpec((GROUP * n, 8, width // 8), lambda i: (i + steps, 0, 0)),
            hbm,
            vmem,
        ],
        out_specs=[vmem, vmem],
        scratch_shapes=[pltpu.VMEM(((rows + CAP) * 8, LANES), F32), pltpu.SemaphoreType.DMA],
    )(row_table, token_table, weight_table, all_grad, early, other_part[0, :, :LANES])

    query_weight_grad, mine = call(
        sum_kernel,
        (shape((8, width), F32), shape((chips, 8, 2 * half), BF16)),
        in_specs=[vmem, vmem],
        limit=16,
    )(arrived, late_done)
    first_key_grad, second_key_grad = call(
        functools.partial(keys_kernel, heads),
        (shape(first_keys.shape, F32), shape(second_keys.shape, F32)),
        in_specs=[vmem, vmem, smem],
        scratch_shapes=[pltpu.VMEM((chips // 4, 2, 2, 8, half), F32)],
        limit=16,
    )(mine, swap_core(mine), core)
    return (
        token_grad,
        query_weight_grad,
        gain_grad,
        shift_grad,
        first_key_grad,
        second_key_grad,
        value_grad.reshape(heads, rows_dev, width),
    )


def solution(mesh):
    fine = Mesh(mesh.devices.reshape(4, 4, 4, 2), ALL)
    split_rows = P(ALL, None)
    in_specs = (
        split_rows, split_rows, P(), P(), P(), P(), P(), P(None, ALL, None),
        P(ALL, None, None), P(ALL, None, None), P(ALL, None, None),
    )
    out_specs = (split_rows, split_rows, P(), P(), P(), P(), P(None, ALL, None))
    return jax.shard_map(per_device, mesh=fine, in_specs=in_specs, out_specs=out_specs, check_vma=False)
```

```python
import functools
import jax
import jax.numpy as jnp
from jax import lax
from jax.experimental import pallas as pl
from jax.experimental.pallas import tpu as pltpu
from jax.sharding import Mesh, PartitionSpec as P

epsilon = 1e-05
F32, BF16, I32 = jnp.float32, jnp.bfloat16, jnp.int32
ALL = ("x", "z", "y", "c")
CHIPS = ("x", "z", "y")
CAP = 40
GROUP = 8
BLOCK = 1024
LANES = 128
NT = (((1,), (1,)), ((), ()))
TN = (((0,), (0,)), ((), ()))


def iota(shape, axis):
    return lax.broadcasted_iota(I32, shape, axis)


def slot_table(pos, payload):
    lines = []
    for j in range(CAP):
        found = sum(jnp.where(p == j, v, jnp.zeros_like(v)) for p, v in zip(pos, payload))
        lines.append(jnp.sum(found, axis=0, keepdims=True))
    lines.append(jnp.zeros((LANES - CAP, LANES), payload[0].dtype))
    return lines


def slots_kernel(heads, top, id_ref, place_ref, pos_ref, dense_ref, slot_ref):
    n = id_ref.shape[0]
    codes = heads * top
    offset = place_ref[0]
    lane = iota((n, LANES), 1)
    row = iota((n, LANES), 0)
    below = (iota((n, n), 1) < iota((n, n), 0)).astype(BF16)
    before = jnp.zeros((1, LANES), F32)
    pos, packed = [], []
    for h in range(heads):
        code = jnp.full((n, LANES), -1, I32)
        for k in range(top):
            at = h * top + k
            shard, own = id_ref[:, at : at + 1], id_ref[:, codes + at : codes + at + 1]
            code = jnp.where(shard == lane, own, code)
        hit = code >= 0
        ones = jnp.where(hit, 1.0, 0.0)
        place = jnp.dot(below, ones.astype(BF16), preferred_element_type=F32) + before
        before = before + jnp.sum(ones, axis=0, keepdims=True)
        place = jnp.where(hit, place, -1.0)
        pos.append(place)
        packed.append(((h * 2048 + code) * BLOCK + offset + row + 1).astype(F32))
        pos_ref[h * n : (h + 1) * n, :] = place
        dense_ref[h * n : (h + 1) * n, :] = code
    table = jnp.concatenate(slot_table(pos, packed)[:CAP], axis=0).astype(I32) - 1
    table = jnp.where(table < 0, (heads * 2048 + iota((CAP, LANES), 0)) * BLOCK, table)
    clash = jnp.zeros((8, LANES), I32)
    for b in range(CAP // 8):
        target = table[b * 8 : b * 8 + 8, :] >> 10
        for d in range(1, 5):
            clash = jnp.where(pltpu.roll(target, d, 0) == target, 1, clash)
    clash = jnp.max(clash.astype(F32), axis=0, keepdims=True) * BLOCK
    rest = jnp.zeros((LANES - CAP - 1, LANES), F32)
    slot_ref[...] = jnp.concatenate([table.astype(F32), clash, rest], axis=0).T.astype(I32)


def score_kernel(
    heads, half, raw_ref, stat_ref, gain_ref, shift_ref, first_ref, second_ref, pos_ref, dense_ref,
    query_ref, normed_ref, state_ref, slot_ref,
):
    n = raw_ref.shape[0]
    normed = (raw_ref[...] - stat_ref[0:1, :]) * stat_ref[1:2, :]
    normed_ref[...] = normed
    query = (normed * gain_ref[...] + shift_ref[...]).astype(BF16)
    query_ref[...] = query
    pos, weights = [], []
    for h in range(heads):
        code = dense_ref[h * n : (h + 1) * n, :]
        hit = code >= 0
        low = code >> 9
        second = jnp.maximum(code, 0) & 511
        base = h * 2 * half
        near = query[:, base : base + half]
        far = query[:, base + half : base + 2 * half]
        score = jnp.zeros((n, LANES), F32)
        for part in range(4):
            dense = lax.dot_general(
                near, first_ref[h, part * LANES : (part + 1) * LANES, :], NT, preferred_element_type=F32
            )
            score = jnp.where(low == part, dense, score)
        found = jnp.zeros((n, LANES), F32)
        for part in range(4):
            dense = lax.dot_general(
                far, second_ref[h, part * LANES : (part + 1) * LANES, :], NT, preferred_element_type=F32
            )
            taken = jnp.take_along_axis(dense, second & (LANES - 1), axis=1)
            found = jnp.where((second >> 7) == part, taken, found)
        score = jnp.where(hit, score + found, -jnp.inf)
        most = jnp.max(score, axis=1, keepdims=True)
        power = jnp.where(hit, jnp.exp(score - most), 0.0)
        weight = power / jnp.sum(power, axis=1, keepdims=True)
        pos.append(pos_ref[h * n : (h + 1) * n, :])
        state_ref[3 * h * n : (3 * h + 1) * n, :] = pos[h]
        state_ref[(3 * h + 1) * n : (3 * h + 2) * n, :] = weight
        state_ref[(3 * h + 2) * n : (3 * h + 3) * n, :] = code.astype(F32)
        weights.append(weight)
    slot_ref[...] = jnp.concatenate(slot_table(pos, weights), axis=0).T


def slot_of(row_ref, token_ref, weight_ref, grad_ref, sender, j):
    grad = grad_ref[token_ref[sender, j]].astype(F32)
    message = (grad * weight_ref[sender, j]).astype(BF16).astype(F32)
    return row_ref[sender, j], message


def product_kernel(row_ref, token_ref, weight_ref, grad_ref, value_ref, product_ref, held):
    step = pl.program_id(0)
    eye = iota((CAP, LANES), 0) == iota((CAP, LANES), 1)

    def one_sender(g, carry):
        for j in range(CAP):
            row, message = slot_of(row_ref, token_ref, weight_ref, grad_ref, step * GROUP + g, j)
            value = value_ref[row].astype(F32)
            held[pl.ds(pl.multiple_of((g * CAP + j) * 8, 8), 8), :] = message * value
        return carry

    lax.fori_loop(0, GROUP, one_sender, 0)
    for g in range(GROUP):
        part = held[pl.ds(g * CAP * 8, CAP, stride=8), :]
        for c in range(1, 8):
            part = part + held[pl.ds(g * CAP * 8 + c, CAP, stride=8), :]
        summed = jnp.sum(part, axis=1, keepdims=True)
        product_ref[g : g + 1, :] = jnp.sum(jnp.where(eye, summed, 0.0), axis=0, keepdims=True)


def spot(row):
    return pl.ds(pl.multiple_of(row * 8, 8), 8)


def add_messages(first, row_ref, token_ref, weight_ref, grad_ref, total):
    def one_sender(g, carry):
        sender = first + g
        clash = row_ref[sender, CAP]

        @pl.when(clash == 0)
        def _():
            for b in range(CAP // 8):
                slots = [
                    slot_of(row_ref, token_ref, weight_ref, grad_ref, sender, b * 8 + u) for u in range(8)
                ]
                sums = [total[spot(row), :] + message for row, message in slots]
                for (row, _), value in zip(slots, sums):
                    total[spot(row), :] = value

        @pl.when(clash != 0)
        def _():
            def one(j, inner):
                row, message = slot_of(row_ref, token_ref, weight_ref, grad_ref, sender, j)
                total[spot(row), :] += message
                return inner

            lax.fori_loop(0, CAP, one, 0)

        return carry

    lax.fori_loop(0, GROUP, one_sender, 0)


def clear_all(total):
    def clear(i, carry):
        at = pl.multiple_of(i * 352, 8)
        total[pl.ds(at, 352), :] = jnp.zeros((352, LANES), F32)
        return carry

    lax.fori_loop(0, total.shape[0] // 352, clear, 0)


def early_kernel(row_ref, token_ref, weight_ref, grad_ref, after_ref, total, done_ref):
    step = pl.program_id(0)
    done_ref[...] = jnp.zeros((8, LANES), F32)

    @pl.when(step == 0)
    def _():
        clear_all(total)

    add_messages(step * GROUP, row_ref, token_ref, weight_ref, grad_ref, total)


def late_kernel(
    senders, steps, row_ref, token_ref, weight_ref, grad_ref, early_ref, after_ref, out_ref, done_ref, total, sem
):
    step = pl.program_id(0)
    done_ref[...] = jnp.zeros((8, LANES), F32)

    @pl.when(step == 0)
    def _():
        copy = pltpu.make_async_copy(early_ref, total, sem)
        copy.start()
        copy.wait()

    @pl.when(step < steps)
    def _():
        add_messages(senders + step * GROUP, row_ref, token_ref, weight_ref, grad_ref, total)

    @pl.when(step >= steps)
    def _():
        lines = out_ref.shape[0]
        first = (step - steps) * lines * 8

        def emit(i, carry):
            for u in range(4):
                at = pl.multiple_of(i * 64 + u * 16, 16)
                for c in range(8):
                    out_ref[pl.ds(at, 16), c * LANES : (c + 1) * LANES] = total[
                        pl.ds(first + at * 8 + c, 16, stride=8), :
                    ].astype(BF16)
            return carry

        lax.fori_loop(0, lines // 64, emit, 0)


def split(value):
    high = value.astype(BF16)
    return high, (value - high.astype(F32)).astype(BF16)


def back_kernel(
    heads, top, half, back_ref, id_ref, state_ref, query_ref,
    normed_ref, first_ref, second_ref, core_ref, grad_ref, own_ref, other_ref, sum_ref, held,
):
    n = query_ref.shape[0]
    core = core_ref[0]
    table = back_ref[...].T
    wide = iota((n, 4 * LANES), 1)
    for h in range(heads):
        pos = state_ref[3 * h * n : (3 * h + 1) * n, :]
        product = jnp.zeros((n, LANES), F32)
        for j in range(CAP):
            product = jnp.where(pos == j, table[j : j + 1, :], product)
        weight = state_ref[(3 * h + 1) * n : (3 * h + 2) * n, :]
        score = product - weight * jnp.sum(product, axis=1, keepdims=True)
        code = state_ref[(3 * h + 2) * n : (3 * h + 3) * n, :].astype(I32)
        low = code >> 9
        near_dense = jnp.concatenate([jnp.where(low == part, score, 0.0) for part in range(4)], axis=1)
        shards = jnp.concatenate(
            [id_ref[:, h * top : (h + 1) * top], jnp.zeros((n, LANES - top), I32)], axis=1
        )
        picked = jnp.take_along_axis(score, shards, axis=1)
        far_dense = jnp.zeros((n, 4 * LANES), F32)
        for k in range(top):
            at = (heads + h) * top + k
            far_dense = far_dense + jnp.where(
                (id_ref[:, at : at + 1] & 511) == wide, picked[:, k : k + 1], 0.0
            )
        base = h * 2 * half
        for side, dense, keys in ((0, near_dense, first_ref), (1, far_dense, second_ref)):
            cols = slice(base + side * half, base + (side + 1) * half)
            high, rest = split(dense)
            table_h = keys[h]
            grad = jnp.dot(high, table_h, preferred_element_type=F32) + jnp.dot(
                rest, table_h, preferred_element_type=F32
            )
            grad_ref[:, cols] = grad
            at = h * 2 + side
            sum_ref[at : at + 1, :] = jnp.sum(grad, axis=0, keepdims=True)
            sum_ref[at + 4 : at + 5, :] = jnp.sum(grad * normed_ref[:, cols], axis=0, keepdims=True)
            query = query_ref[:, cols]
            keys_grad = lax.dot_general(high, query, TN, preferred_element_type=F32) + lax.dot_general(
                rest, query, TN, preferred_element_type=F32
            )
            blocks = keys_grad.reshape(16, 2, 2, 8, half)
            first = (side * heads + h) * 16
            held[first : first + 16, :, :, 0:half] = blocks[:, :, 0]
            held[first : first + 16, :, :, half : 2 * half] = blocks[:, :, 1]
    own_ref[...] = held[:, core]
    other_ref[...] = held[:, 1 - core]


def tail_kernel(
    everything, arrived_ref, query_grad_ref, normed_ref, gain_ref, stat_ref, tokens_ref, core_ref, after_ref,
    raw_ref, own_ref, other_ref, sum_ref, block_ref, held,
):
    core = core_ref[0]
    half = 256
    reduced = jnp.sum(arrived_ref[...], axis=0)
    block_ref[...] = reduced[:, half:].astype(BF16)
    shift_sum = jnp.concatenate([reduced[i : i + 1, :half] for i in range(4)], axis=1)
    gain_sum = jnp.concatenate([reduced[i : i + 1, :half] for i in range(4, 8)], axis=1)
    sum_ref[0:1, :] = shift_sum
    sum_ref[1:2, :] = gain_sum
    raw_grad = (
        gain_ref[...]
        * stat_ref[1:2, :]
        * (query_grad_ref[...] - shift_sum / everything - normed_ref[...] * gain_sum / everything)
    ).astype(BF16)
    raw_ref[...] = raw_grad
    part = lax.dot_general(raw_grad, tokens_ref[...], TN, preferred_element_type=F32)
    held[...] = part.reshape(held.shape)
    own_ref[...] = held[:, core]
    other_ref[...] = held[:, 1 - core]


def sum_kernel(arrived_ref, after_ref, sum_ref, mine_ref):
    width = sum_ref.shape[1]
    sum_ref[...] = jnp.sum(arrived_ref[:, :, :width].astype(F32), axis=0)
    mine_ref[...] = arrived_ref[:, :, width:]


def keys_kernel(heads, mine_ref, theirs_ref, core_ref, first_ref, second_ref, held):
    subkeys, half = first_ref.shape[1:]
    at_zero = core_ref[0] == 0
    each = subkeys // 32
    source = iota((subkeys, subkeys), 0)
    source = (source & 3) * LANES + (source >> 2)
    order = (iota((subkeys, subkeys), 1) == source).astype(BF16)
    for side in range(2):
        for h in range(heads):
            at = (side * heads + h) * each
            mine = mine_ref[at : at + each].astype(F32)
            theirs = theirs_ref[at : at + each].astype(F32)
            pair = (jnp.where(at_zero, mine, theirs), jnp.where(at_zero, theirs, mine))
            for c in range(2):
                held[:, c, 0] = pair[c][:, :, :half]
                held[:, c, 1] = pair[c][:, :, half:]
            keys = held[...].reshape(subkeys, half)
            if side == 0:
                first_ref[h] = jnp.dot(order, keys.astype(BF16), preferred_element_type=F32)
            else:
                second_ref[h] = keys


def call(kernel, out_shape, limit=16, **more):
    return pl.pallas_call(
        kernel,
        out_shape=out_shape,
        compiler_params=pltpu.CompilerParams(vmem_limit_bytes=limit << 20),
        **more,
    )


def shape(dims, dtype):
    return jax.ShapeDtypeStruct(dims, dtype)


def swap_core(value):
    return lax.ppermute(value, "c", [(0, 1), (1, 0)])


def everyone(value, axis):
    size = lax.axis_size(axis)
    wide = jnp.broadcast_to(value[None], (size,) + value.shape)
    return lax.all_to_all(wide, axis, split_axis=0, concat_axis=0, tiled=True)


def all_moments(mean, spread, count):
    for axis in ("c", "y", "z", "x"):
        both = jnp.stack([mean, spread])
        parts = jnp.stack([both, swap_core(both)]) if axis == "c" else everyone(both, axis)
        mean = jnp.mean(parts[:, 0], axis=0)
        spread = jnp.sum(parts[:, 1] + count * jnp.square(parts[:, 0] - mean), axis=0)
        count = count * parts.shape[0]
    return mean, spread / count


def exchange(value, axis):
    return lax.all_to_all(value, axis, split_axis=0, concat_axis=0, tiled=True)


def per_device(
    tokens, out_grad, query_weight, gain, shift, first_keys, second_keys, values, pick_shard, pick_low,
    pick_second,
):
    devices = lax.axis_size(ALL)
    n = tokens.shape[0]
    heads, rows_dev, width = values.shape
    subkeys, half = first_keys.shape[1:]
    top = pick_shard.shape[2]
    everything = n * devices
    rows = heads * rows_dev

    tiles = out_grad.reshape(n, 8, width // 8)
    all_grad = lax.all_gather(tiles, ALL, axis=0, tiled=True)

    raw_query = jnp.dot(tokens, query_weight, preferred_element_type=F32)
    local_mean = jnp.mean(raw_query, axis=0)
    local_spread = jnp.sum(jnp.square(raw_query - local_mean), axis=0)
    centre, spread = all_moments(local_mean, local_spread, n)
    inverse = 1.0 / jnp.sqrt(spread + epsilon)

    stats = jnp.stack([centre, inverse])
    shard_ids = pick_shard.reshape(n, heads * top)
    second_ids = pick_second.reshape(n, heads * top)
    code = pick_low.reshape(n, heads * top) * subkeys + second_ids
    ids = jnp.concatenate([shard_ids, code], axis=1)
    vmem = pl.BlockSpec(memory_space=pltpu.VMEM)
    smem = pl.BlockSpec(memory_space=pltpu.SMEM)
    hbm = pl.BlockSpec(memory_space=pltpu.HBM)
    place = jnp.reshape(lax.axis_index(ALL) % GROUP * n, (1,)).astype(I32)
    pos, dense, slot_index = call(
        functools.partial(slots_kernel, heads, top),
        (shape((heads * n, LANES), F32), shape((heads * n, LANES), I32), shape((devices, LANES), I32)),
        in_specs=[vmem, smem],
    )(ids, place)
    slot_index = lax.all_to_all(slot_index.reshape(devices, 1, LANES), ALL, split_axis=0, concat_axis=0, tiled=True)

    first_split = first_keys.reshape(heads, devices, subkeys // devices, half).swapaxes(1, 2)
    first_split = first_split.reshape(heads, subkeys, half)
    query, normed, state, slot_weight = call(
        functools.partial(score_kernel, heads, half),
        (
            shape((n, width), BF16),
            shape((n, width), F32),
            shape((3 * heads * n, LANES), F32),
            shape((devices, LANES), F32),
        ),
    )(
        raw_query, stats, gain[None], shift[None], first_split, second_keys, pos, dense
    )
    slot_weight = lax.all_to_all(slot_weight.reshape(devices, 1, LANES), ALL, split_axis=0, concat_axis=0, tiled=True)

    value_tiles = values.reshape(rows, 8, width // 8)
    slot_index = slot_index.reshape(devices, LANES)
    row_table = slot_index >> 10
    token_table = slot_index & (BLOCK - 1)
    weight_table = slot_weight.reshape(devices, LANES)
    grad_spec = pl.BlockSpec((GROUP * n, 8, width // 8), lambda i: (i, 0, 0))
    product = call(
        product_kernel,
        shape((devices, LANES), F32),
        limit=28,
        grid=(devices // GROUP,),
        in_specs=[smem, smem, smem, grad_spec, vmem],
        out_specs=pl.BlockSpec((GROUP, LANES), lambda i: (i, 0)),
        scratch_shapes=[pltpu.VMEM((GROUP * CAP * 8, LANES), F32)],
    )(row_table & (rows - 1), token_table, weight_table, all_grad, value_tiles)
    returned = exchange(product.reshape(devices, 1, LANES), ALL)

    chips = devices // 2
    core = jnp.reshape(lax.axis_index("c"), (1,)).astype(I32)
    query_grad, own_keys, other_keys, sums = call(
        functools.partial(back_kernel, heads, top, half),
        (
            shape((n, width), F32),
            shape((chips, 8, 2 * half), F32),
            shape((chips, 8, 2 * half), F32),
            shape((8, half), F32),
        ),
        in_specs=[vmem] * 7 + [smem],
        scratch_shapes=[pltpu.VMEM((chips, 2, 8, 2 * half), F32)],
    )(
        returned.reshape(devices, LANES), ids, state, query, normed,
        first_split, second_keys, core,
    )
    keys_in, sums_in = swap_core((other_keys, sums))
    sums = jnp.broadcast_to((sums + sums_in)[None], (chips, 8, half))
    sent = jnp.concatenate([sums, own_keys + keys_in], axis=2)
    arrived = exchange(sent, CHIPS)
    steps = 9
    rest = devices // GROUP - steps
    early, early_done = call(
        early_kernel,
        (shape(((rows + CAP) * 8, LANES), F32), shape((8, LANES), F32)),
        limit=32,
        grid=(steps,),
        in_specs=[smem, smem, smem, grad_spec, vmem],
        out_specs=[vmem, vmem],
    )(row_table, token_table, weight_table, all_grad, sent[0, :, :LANES])

    raw_grad, own_part, other_part, sums, key_block = call(
        functools.partial(tail_kernel, everything),
        (
            shape((n, width), BF16),
            shape((chips, 8, width), F32),
            shape((chips, 8, width), F32),
            shape((2, width), F32),
            shape((8, 2 * half), BF16),
        ),
        in_specs=[vmem] * 6 + [smem, vmem],
        scratch_shapes=[pltpu.VMEM((chips, 2, 8, width), F32)],
        limit=24,
    )(arrived, query_grad, normed, gain[None], stats, tokens, core, early_done)
    shift_grad, gain_grad = sums
    other_part = swap_core(other_part)
    own_part = (own_part + other_part).astype(BF16)
    key_wide = jnp.broadcast_to(key_block[None], (chips, 8, 2 * half))
    sent = jnp.concatenate([own_part, key_wide], axis=2)
    arrived = exchange(sent, CHIPS)
    token_grad = lax.dot_general(raw_grad, query_weight, NT, preferred_element_type=F32).astype(BF16)
    lines = 512
    value_grad, late_done = call(
        functools.partial(late_kernel, steps * GROUP, rest),
        (shape((rows, width), BF16), shape((8, LANES), F32)),
        limit=50,
        grid=(rest + rows // lines,),
        in_specs=[
            smem,
            smem,
            smem,
            pl.BlockSpec((GROUP * n, 8, width // 8), lambda i: (jnp.minimum(i, rest - 1) + steps, 0, 0)),
            hbm,
            vmem,
        ],
        out_specs=[pl.BlockSpec((lines, width), lambda i: (jnp.maximum(i - rest, 0), 0)), vmem],
        scratch_shapes=[pltpu.VMEM(((rows + CAP) * 8, LANES), F32), pltpu.SemaphoreType.DMA],
    )(row_table, token_table, weight_table, all_grad, early, other_part[0, :, :LANES])

    query_weight_grad, mine = call(
        sum_kernel,
        (shape((8, width), F32), shape((chips, 8, 2 * half), BF16)),
        in_specs=[vmem, vmem],
        limit=16,
    )(arrived, late_done)
    first_key_grad, second_key_grad = call(
        functools.partial(keys_kernel, heads),
        (shape(first_keys.shape, F32), shape(second_keys.shape, F32)),
        in_specs=[vmem, vmem, smem],
        scratch_shapes=[pltpu.VMEM((chips // 4, 2, 2, 8, half), F32)],
        limit=16,
    )(mine, swap_core(mine), core)
    return (
        token_grad,
        query_weight_grad,
        gain_grad,
        shift_grad,
        first_key_grad,
        second_key_grad,
        value_grad.reshape(heads, rows_dev, width),
    )


def solution(mesh):
    fine = Mesh(mesh.devices.reshape(4, 4, 4, 2), ALL)
    split_rows = P(ALL, None)
    in_specs = (
        split_rows, split_rows, P(), P(), P(), P(), P(), P(None, ALL, None),
        P(ALL, None, None), P(ALL, None, None), P(ALL, None, None),
    )
    out_specs = (split_rows, split_rows, P(), P(), P(), P(), P(None, ALL, None))
    return jax.shard_map(per_device, mesh=fine, in_specs=in_specs, out_specs=out_specs, check_vma=False)
```

```python
import functools
import jax
import jax.numpy as jnp
from jax import lax
from jax.experimental import pallas as pl
from jax.experimental.pallas import tpu as pltpu
from jax.sharding import Mesh, PartitionSpec as P

epsilon = 1e-05
F32, BF16, I32 = jnp.float32, jnp.bfloat16, jnp.int32
ALL = ("x", "z", "y", "c")
CHIPS = ("x", "z", "y")
CAP = 40
GROUP = 8
BLOCK = 1024
LANES = 128
NT = (((1,), (1,)), ((), ()))
TN = (((0,), (0,)), ((), ()))


def iota(shape, axis):
    return lax.broadcasted_iota(I32, shape, axis)


def slot_table(pos, payload):
    lines = []
    for j in range(CAP):
        found = sum(jnp.where(p == j, v, jnp.zeros_like(v)) for p, v in zip(pos, payload))
        lines.append(jnp.sum(found, axis=0, keepdims=True))
    lines.append(jnp.zeros((LANES - CAP, LANES), payload[0].dtype))
    return lines


def slots_kernel(heads, top, id_ref, place_ref, pos_ref, dense_ref, slot_ref):
    n = id_ref.shape[0]
    codes = heads * top
    offset = place_ref[0]
    lane = iota((n, LANES), 1)
    row = iota((n, LANES), 0)
    below = (iota((n, n), 1) < iota((n, n), 0)).astype(BF16)
    before = jnp.zeros((1, LANES), F32)
    pos, packed = [], []
    for h in range(heads):
        code = jnp.full((n, LANES), -1, I32)
        for k in range(top):
            at = h * top + k
            shard, own = id_ref[:, at : at + 1], id_ref[:, codes + at : codes + at + 1]
            code = jnp.where(shard == lane, own, code)
        hit = code >= 0
        ones = jnp.where(hit, 1.0, 0.0)
        place = jnp.dot(below, ones.astype(BF16), preferred_element_type=F32) + before
        before = before + jnp.sum(ones, axis=0, keepdims=True)
        place = jnp.where(hit, place, -1.0)
        pos.append(place)
        packed.append(((h * 2048 + code) * BLOCK + offset + row + 1).astype(F32))
        pos_ref[h * n : (h + 1) * n, :] = place
        dense_ref[h * n : (h + 1) * n, :] = code
    table = jnp.concatenate(slot_table(pos, packed)[:CAP], axis=0).astype(I32) - 1
    table = jnp.where(table < 0, (heads * 2048 + iota((CAP, LANES), 0)) * BLOCK, table)
    clash = jnp.zeros((8, LANES), I32)
    for b in range(CAP // 8):
        target = table[b * 8 : b * 8 + 8, :] >> 10
        for d in range(1, 5):
            clash = jnp.where(pltpu.roll(target, d, 0) == target, 1, clash)
    clash = jnp.max(clash.astype(F32), axis=0, keepdims=True) * BLOCK
    rest = jnp.zeros((LANES - CAP - 1, LANES), F32)
    slot_ref[...] = jnp.concatenate([table.astype(F32), clash, rest], axis=0).T.astype(I32)


def score_kernel(
    heads, half, raw_ref, stat_ref, gain_ref, shift_ref, first_ref, second_ref, pos_ref, dense_ref,
    query_ref, normed_ref, state_ref, slot_ref,
):
    n = raw_ref.shape[0]
    normed = (raw_ref[...] - stat_ref[0:1, :]) * stat_ref[1:2, :]
    normed_ref[...] = normed
    query = (normed * gain_ref[...] + shift_ref[...]).astype(BF16)
    query_ref[...] = query
    pos, weights = [], []
    for h in range(heads):
        code = dense_ref[h * n : (h + 1) * n, :]
        hit = code >= 0
        low = code >> 9
        second = jnp.maximum(code, 0) & 511
        base = h * 2 * half
        near = query[:, base : base + half]
        far = query[:, base + half : base + 2 * half]
        score = jnp.zeros((n, LANES), F32)
        for part in range(4):
            dense = lax.dot_general(
                near, first_ref[h, part * LANES : (part + 1) * LANES, :], NT, preferred_element_type=F32
            )
            score = jnp.where(low == part, dense, score)
        found = jnp.zeros((n, LANES), F32)
        for part in range(4):
            dense = lax.dot_general(
                far, second_ref[h, part * LANES : (part + 1) * LANES, :], NT, preferred_element_type=F32
            )
            taken = jnp.take_along_axis(dense, second & (LANES - 1), axis=1)
            found = jnp.where((second >> 7) == part, taken, found)
        score = jnp.where(hit, score + found, -jnp.inf)
        most = jnp.max(score, axis=1, keepdims=True)
        power = jnp.where(hit, jnp.exp(score - most), 0.0)
        weight = power / jnp.sum(power, axis=1, keepdims=True)
        pos.append(pos_ref[h * n : (h + 1) * n, :])
        state_ref[3 * h * n : (3 * h + 1) * n, :] = pos[h]
        state_ref[(3 * h + 1) * n : (3 * h + 2) * n, :] = weight
        state_ref[(3 * h + 2) * n : (3 * h + 3) * n, :] = code.astype(F32)
        weights.append(weight)
    slot_ref[...] = jnp.concatenate(slot_table(pos, weights), axis=0).T


def slot_of(row_ref, token_ref, weight_ref, grad_ref, sender, j):
    grad = grad_ref[token_ref[sender, j]].astype(F32)
    message = (grad * weight_ref[sender, j]).astype(BF16).astype(F32)
    return row_ref[sender, j], message


def product_kernel(row_ref, token_ref, weight_ref, grad_ref, value_ref, product_ref, held):
    step = pl.program_id(0)
    eye = iota((CAP, LANES), 0) == iota((CAP, LANES), 1)

    def one_sender(g, carry):
        for j in range(CAP):
            row, message = slot_of(row_ref, token_ref, weight_ref, grad_ref, step * GROUP + g, j)
            value = value_ref[row].astype(F32)
            held[pl.ds(pl.multiple_of((g * CAP + j) * 8, 8), 8), :] = message * value
        return carry

    lax.fori_loop(0, GROUP, one_sender, 0)
    for g in range(GROUP):
        part = held[pl.ds(g * CAP * 8, CAP, stride=8), :]
        for c in range(1, 8):
            part = part + held[pl.ds(g * CAP * 8 + c, CAP, stride=8), :]
        summed = jnp.sum(part, axis=1, keepdims=True)
        product_ref[g : g + 1, :] = jnp.sum(jnp.where(eye, summed, 0.0), axis=0, keepdims=True)


def spot(row):
    return pl.ds(pl.multiple_of(row * 8, 8), 8)


def add_messages(first, row_ref, token_ref, weight_ref, grad_ref, total):
    def one_sender(g, carry):
        sender = first + g
        clash = row_ref[sender, CAP]

        @pl.when(clash == 0)
        def _():
            for b in range(CAP // 8):
                slots = [
                    slot_of(row_ref, token_ref, weight_ref, grad_ref, sender, b * 8 + u) for u in range(8)
                ]
                sums = [total[spot(row), :] + message for row, message in slots]
                for (row, _), value in zip(slots, sums):
                    total[spot(row), :] = value

        @pl.when(clash != 0)
        def _():
            def one(j, inner):
                row, message = slot_of(row_ref, token_ref, weight_ref, grad_ref, sender, j)
                total[spot(row), :] += message
                return inner

            lax.fori_loop(0, CAP, one, 0)

        return carry

    lax.fori_loop(0, GROUP, one_sender, 0)


def clear_all(total):
    def clear(i, carry):
        at = pl.multiple_of(i * 352, 8)
        total[pl.ds(at, 352), :] = jnp.zeros((352, LANES), F32)
        return carry

    lax.fori_loop(0, total.shape[0] // 352, clear, 0)


def early_kernel(row_ref, token_ref, weight_ref, grad_ref, after_ref, total, done_ref):
    step = pl.program_id(0)
    done_ref[...] = jnp.zeros((8, LANES), F32)

    @pl.when(step == 0)
    def _():
        clear_all(total)

    add_messages(step * GROUP, row_ref, token_ref, weight_ref, grad_ref, total)


def late_kernel(
    senders, steps, row_ref, token_ref, weight_ref, grad_ref, early_ref, after_ref, out_ref, done_ref, total, sem
):
    step = pl.program_id(0)
    done_ref[...] = jnp.zeros((8, LANES), F32)

    @pl.when(step == 0)
    def _():
        copy = pltpu.make_async_copy(early_ref, total, sem)
        copy.start()
        copy.wait()

    @pl.when(step < steps)
    def _():
        add_messages(senders + step * GROUP, row_ref, token_ref, weight_ref, grad_ref, total)

    @pl.when(step >= steps)
    def _():
        lines = out_ref.shape[0]
        first = (step - steps) * lines * 8

        def emit(i, carry):
            for u in range(4):
                at = pl.multiple_of(i * 64 + u * 16, 16)
                for c in range(8):
                    out_ref[pl.ds(at, 16), c * LANES : (c + 1) * LANES] = total[
                        pl.ds(first + at * 8 + c, 16, stride=8), :
                    ].astype(BF16)
            return carry

        lax.fori_loop(0, lines // 64, emit, 0)


def split(value):
    high = value.astype(BF16)
    return high, (value - high.astype(F32)).astype(BF16)


def back_kernel(
    heads, top, half, back_ref, id_ref, state_ref, query_ref,
    normed_ref, first_ref, second_ref, core_ref, grad_ref, own_ref, other_ref, sum_ref, held,
):
    n = query_ref.shape[0]
    core = core_ref[0]
    table = back_ref[...].T
    wide = iota((n, 4 * LANES), 1)
    for h in range(heads):
        pos = state_ref[3 * h * n : (3 * h + 1) * n, :]
        product = jnp.zeros((n, LANES), F32)
        for j in range(CAP):
            product = jnp.where(pos == j, table[j : j + 1, :], product)
        weight = state_ref[(3 * h + 1) * n : (3 * h + 2) * n, :]
        score = product - weight * jnp.sum(product, axis=1, keepdims=True)
        code = state_ref[(3 * h + 2) * n : (3 * h + 3) * n, :].astype(I32)
        low = code >> 9
        near_dense = jnp.concatenate([jnp.where(low == part, score, 0.0) for part in range(4)], axis=1)
        shards = jnp.concatenate(
            [id_ref[:, h * top : (h + 1) * top], jnp.zeros((n, LANES - top), I32)], axis=1
        )
        picked = jnp.take_along_axis(score, shards, axis=1)
        far_dense = jnp.zeros((n, 4 * LANES), F32)
        for k in range(top):
            at = (heads + h) * top + k
            far_dense = far_dense + jnp.where(
                (id_ref[:, at : at + 1] & 511) == wide, picked[:, k : k + 1], 0.0
            )
        base = h * 2 * half
        for side, dense, keys in ((0, near_dense, first_ref), (1, far_dense, second_ref)):
            cols = slice(base + side * half, base + (side + 1) * half)
            high, rest = split(dense)
            table_h = keys[h]
            grad = jnp.dot(high, table_h, preferred_element_type=F32) + jnp.dot(
                rest, table_h, preferred_element_type=F32
            )
            grad_ref[:, cols] = grad
            at = h * 2 + side
            sum_ref[at : at + 1, :] = jnp.sum(grad, axis=0, keepdims=True)
            sum_ref[at + 4 : at + 5, :] = jnp.sum(grad * normed_ref[:, cols], axis=0, keepdims=True)
            query = query_ref[:, cols]
            keys_grad = lax.dot_general(high, query, TN, preferred_element_type=F32) + lax.dot_general(
                rest, query, TN, preferred_element_type=F32
            )
            blocks = keys_grad.reshape(16, 2, 2, 8, half)
            first = (side * heads + h) * 16
            held[first : first + 16, :, :, 0:half] = blocks[:, :, 0]
            held[first : first + 16, :, :, half : 2 * half] = blocks[:, :, 1]
    own_ref[...] = held[:, core]
    other_ref[...] = held[:, 1 - core]


def tail_kernel(
    everything, arrived_ref, query_grad_ref, normed_ref, gain_ref, stat_ref, tokens_ref, core_ref, after_ref,
    raw_ref, own_ref, other_ref, sum_ref, block_ref, held,
):
    core = core_ref[0]
    half = 256
    reduced = jnp.sum(arrived_ref[...], axis=0)
    block_ref[...] = reduced[:, half:].astype(BF16)
    shift_sum = jnp.concatenate([reduced[i : i + 1, :half] for i in range(4)], axis=1)
    gain_sum = jnp.concatenate([reduced[i : i + 1, :half] for i in range(4, 8)], axis=1)
    sum_ref[0:1, :] = shift_sum
    sum_ref[1:2, :] = gain_sum
    raw_grad = (
        gain_ref[...]
        * stat_ref[1:2, :]
        * (query_grad_ref[...] - shift_sum / everything - normed_ref[...] * gain_sum / everything)
    ).astype(BF16)
    raw_ref[...] = raw_grad
    part = lax.dot_general(raw_grad, tokens_ref[...], TN, preferred_element_type=F32)
    held[...] = part.reshape(held.shape)
    own_ref[...] = held[:, core]
    other_ref[...] = held[:, 1 - core]


def sum_kernel(arrived_ref, after_ref, sum_ref, mine_ref):
    width = sum_ref.shape[1]
    sum_ref[...] = jnp.sum(arrived_ref[:, :, :width].astype(F32), axis=0)
    mine_ref[...] = arrived_ref[:, :, width:]


def keys_kernel(heads, mine_ref, theirs_ref, core_ref, first_ref, second_ref, held):
    subkeys, half = first_ref.shape[1:]
    at_zero = core_ref[0] == 0
    each = subkeys // 32
    source = iota((subkeys, subkeys), 0)
    source = (source & 3) * LANES + (source >> 2)
    order = (iota((subkeys, subkeys), 1) == source).astype(BF16)
    for side in range(2):
        for h in range(heads):
            at = (side * heads + h) * each
            mine = mine_ref[at : at + each].astype(F32)
            theirs = theirs_ref[at : at + each].astype(F32)
            pair = (jnp.where(at_zero, mine, theirs), jnp.where(at_zero, theirs, mine))
            for c in range(2):
                held[:, c, 0] = pair[c][:, :, :half]
                held[:, c, 1] = pair[c][:, :, half:]
            keys = held[...].reshape(subkeys, half)
            if side == 0:
                first_ref[h] = jnp.dot(order, keys.astype(BF16), preferred_element_type=F32)
            else:
                second_ref[h] = keys


def call(kernel, out_shape, limit=16, **more):
    return pl.pallas_call(
        kernel,
        out_shape=out_shape,
        compiler_params=pltpu.CompilerParams(vmem_limit_bytes=limit << 20),
        **more,
    )


def shape(dims, dtype):
    return jax.ShapeDtypeStruct(dims, dtype)


def swap_core(value):
    return lax.ppermute(value, "c", [(0, 1), (1, 0)])


def everyone(value, axis):
    size = lax.axis_size(axis)
    wide = jnp.broadcast_to(value[None], (size,) + value.shape)
    return lax.all_to_all(wide, axis, split_axis=0, concat_axis=0, tiled=True)


def all_moments(mean, spread, count):
    for axis in ("c", "y", "z", "x"):
        both = jnp.stack([mean, spread])
        parts = jnp.stack([both, swap_core(both)]) if axis == "c" else everyone(both, axis)
        mean = jnp.mean(parts[:, 0], axis=0)
        spread = jnp.sum(parts[:, 1] + count * jnp.square(parts[:, 0] - mean), axis=0)
        count = count * parts.shape[0]
    return mean, spread / count


def exchange(value, axis):
    return lax.all_to_all(value, axis, split_axis=0, concat_axis=0, tiled=True)


def per_device(
    tokens, out_grad, query_weight, gain, shift, first_keys, second_keys, values, pick_shard, pick_low,
    pick_second,
):
    devices = lax.axis_size(ALL)
    n = tokens.shape[0]
    heads, rows_dev, width = values.shape
    subkeys, half = first_keys.shape[1:]
    top = pick_shard.shape[2]
    everything = n * devices
    rows = heads * rows_dev

    tiles = out_grad.reshape(n, 8, width // 8)
    all_grad = lax.all_gather(tiles, ALL, axis=0, tiled=True)

    raw_query = jnp.dot(tokens, query_weight, preferred_element_type=F32)
    local_mean = jnp.mean(raw_query, axis=0)
    local_spread = jnp.sum(jnp.square(raw_query - local_mean), axis=0)
    centre, spread = all_moments(local_mean, local_spread, n)
    inverse = 1.0 / jnp.sqrt(spread + epsilon)

    stats = jnp.stack([centre, inverse])
    shard_ids = pick_shard.reshape(n, heads * top)
    second_ids = pick_second.reshape(n, heads * top)
    code = pick_low.reshape(n, heads * top) * subkeys + second_ids
    ids = jnp.concatenate([shard_ids, code], axis=1)
    vmem = pl.BlockSpec(memory_space=pltpu.VMEM)
    smem = pl.BlockSpec(memory_space=pltpu.SMEM)
    hbm = pl.BlockSpec(memory_space=pltpu.HBM)
    place = jnp.reshape(lax.axis_index(ALL) % GROUP * n, (1,)).astype(I32)
    pos, dense, slot_index = call(
        functools.partial(slots_kernel, heads, top),
        (shape((heads * n, LANES), F32), shape((heads * n, LANES), I32), shape((devices, LANES), I32)),
        in_specs=[vmem, smem],
    )(ids, place)
    slot_index = lax.all_to_all(slot_index.reshape(devices, 1, LANES), ALL, split_axis=0, concat_axis=0, tiled=True)

    first_split = first_keys.reshape(heads, devices, subkeys // devices, half).swapaxes(1, 2)
    first_split = first_split.reshape(heads, subkeys, half)
    query, normed, state, slot_weight = call(
        functools.partial(score_kernel, heads, half),
        (
            shape((n, width), BF16),
            shape((n, width), F32),
            shape((3 * heads * n, LANES), F32),
            shape((devices, LANES), F32),
        ),
    )(
        raw_query, stats, gain[None], shift[None], first_split, second_keys, pos, dense
    )
    slot_weight = lax.all_to_all(slot_weight.reshape(devices, 1, LANES), ALL, split_axis=0, concat_axis=0, tiled=True)

    value_tiles = values.reshape(rows, 8, width // 8)
    slot_index = slot_index.reshape(devices, LANES)
    row_table = slot_index >> 10
    token_table = slot_index & (BLOCK - 1)
    weight_table = slot_weight.reshape(devices, LANES)
    grad_spec = pl.BlockSpec((GROUP * n, 8, width // 8), lambda i: (i, 0, 0))
    product = call(
        product_kernel,
        shape((devices, LANES), F32),
        limit=28,
        grid=(devices // GROUP,),
        in_specs=[smem, smem, smem, grad_spec, vmem],
        out_specs=pl.BlockSpec((GROUP, LANES), lambda i: (i, 0)),
        scratch_shapes=[pltpu.VMEM((GROUP * CAP * 8, LANES), F32)],
    )(row_table & (rows - 1), token_table, weight_table, all_grad, value_tiles)
    returned = exchange(product.reshape(devices, 1, LANES), ALL)

    chips = devices // 2
    core = jnp.reshape(lax.axis_index("c"), (1,)).astype(I32)
    query_grad, own_keys, other_keys, sums = call(
        functools.partial(back_kernel, heads, top, half),
        (
            shape((n, width), F32),
            shape((chips, 8, 2 * half), F32),
            shape((chips, 8, 2 * half), F32),
            shape((8, half), F32),
        ),
        in_specs=[vmem] * 7 + [smem],
        scratch_shapes=[pltpu.VMEM((chips, 2, 8, 2 * half), F32)],
    )(
        returned.reshape(devices, LANES), ids, state, query, normed,
        first_split, second_keys, core,
    )
    keys_in, sums_in = swap_core((other_keys, sums))
    sums = jnp.broadcast_to((sums + sums_in)[None], (chips, 8, half))
    sent = jnp.concatenate([sums, own_keys + keys_in], axis=2)
    arrived = exchange(sent, CHIPS)
    steps = 10
    rest = devices // GROUP - steps
    early, early_done = call(
        early_kernel,
        (shape(((rows + CAP) * 8, LANES), F32), shape((8, LANES), F32)),
        limit=32,
        grid=(steps,),
        in_specs=[smem, smem, smem, grad_spec, vmem],
        out_specs=[vmem, vmem],
    )(row_table, token_table, weight_table, all_grad, sent[0, :, :LANES])

    raw_grad, own_part, other_part, sums, key_block = call(
        functools.partial(tail_kernel, everything),
        (
            shape((n, width), BF16),
            shape((chips, 8, width), F32),
            shape((chips, 8, width), F32),
            shape((2, width), F32),
            shape((8, 2 * half), BF16),
        ),
        in_specs=[vmem] * 6 + [smem, vmem],
        scratch_shapes=[pltpu.VMEM((chips, 2, 8, width), F32)],
        limit=24,
    )(arrived, query_grad, normed, gain[None], stats, tokens, core, early_done)
    shift_grad, gain_grad = sums
    other_part = swap_core(other_part)
    own_part = (own_part + other_part).astype(BF16)
    key_wide = jnp.broadcast_to(key_block[None], (chips, 8, 2 * half))
    sent = jnp.concatenate([own_part, key_wide], axis=2)
    arrived = exchange(sent, CHIPS)
    token_grad = lax.dot_general(raw_grad, query_weight, NT, preferred_element_type=F32).astype(BF16)
    lines = 512
    value_grad, late_done = call(
        functools.partial(late_kernel, steps * GROUP, rest),
        (shape((rows, width), BF16), shape((8, LANES), F32)),
        limit=50,
        grid=(rest + rows // lines,),
        in_specs=[
            smem,
            smem,
            smem,
            pl.BlockSpec((GROUP * n, 8, width // 8), lambda i: (jnp.minimum(i, rest - 1) + steps, 0, 0)),
            hbm,
            vmem,
        ],
        out_specs=[pl.BlockSpec((lines, width), lambda i: (jnp.maximum(i - rest, 0), 0)), vmem],
        scratch_shapes=[pltpu.VMEM(((rows + CAP) * 8, LANES), F32), pltpu.SemaphoreType.DMA],
    )(row_table, token_table, weight_table, all_grad, early, key_wide[0, :, :LANES])

    query_weight_grad, mine = call(
        sum_kernel,
        (shape((8, width), F32), shape((chips, 8, 2 * half), BF16)),
        in_specs=[vmem, vmem],
        limit=16,
    )(arrived, late_done)
    first_key_grad, second_key_grad = call(
        functools.partial(keys_kernel, heads),
        (shape(first_keys.shape, F32), shape(second_keys.shape, F32)),
        in_specs=[vmem, vmem, smem],
        scratch_shapes=[pltpu.VMEM((chips // 4, 2, 2, 8, half), F32)],
        limit=16,
    )(mine, swap_core(mine), core)
    return (
        token_grad,
        query_weight_grad,
        gain_grad,
        shift_grad,
        first_key_grad,
        second_key_grad,
        value_grad.reshape(heads, rows_dev, width),
    )


def solution(mesh):
    fine = Mesh(mesh.devices.reshape(4, 4, 4, 2), ALL)
    split_rows = P(ALL, None)
    in_specs = (
        split_rows, split_rows, P(), P(), P(), P(), P(), P(None, ALL, None),
        P(ALL, None, None), P(ALL, None, None), P(ALL, None, None),
    )
    out_specs = (split_rows, split_rows, P(), P(), P(), P(), P(None, ALL, None))
    return jax.shard_map(per_device, mesh=fine, in_specs=in_specs, out_specs=out_specs, check_vma=False)
```
